32 devices in a mesh: dir: 2 (over x), row: 16 (over z, y, core).
Axes of the slice: x: 2, y: 2, z: 4, core: 2. Of those that a mesh axis runs over, the one named last changes fastest.
Arguments:
- white_noise: bfloat16 [2, 8192, 8192], P(None, ('dir', 'row')), may hold values from -6 to 6
- geometry: int32 [2, 2], P('dir'), may hold values from 0 to 3
- window: int32 [2], P('dir'), may hold values from 1 to 8, as said below
- tile_map: int32 [2, 512], P('dir'), may hold values from 0 to 16383
- link_gain: float32 [2, 512], P('dir'), may hold values from 0.1 to 1
- serving: int32 [512], replicated, may hold values from 0 to 1
Outputs:
- fluctuation: float32 [2, 128, 128], P('dir', 'row')
- signal_ratio: float32 [512], P(('dir', 'row'))
The draws below stay inside these ranges and needn't reach their ends.
Inputs may be any that keep to these rules, and one draw needn't show every extreme that they name: geometry[d,0] is direction d's Fresnel-scale bin and geometry[d,1] its slant bin. `window`: some direction has the half-width 8. `tile_map`: tile (t,u) is numbered t * 128 + u.
All inputs are finite; a program needn't handle non-finite values.
Results may differ from the reference program's by a relative error of at most 0.034.
Values may be sent and summed in bfloat16 or wider, within the bound.
A program may use at most 64 MiB of HBM per device.

```python
import math
import jax
import jax.numpy as jnp
from jax import lax

N = 8192
FIRST = 64
SECOND = 128
ROWS_DEV = 32
PATCH = 512
XTILES = 128
YTILES = 8
TILE_X = 64
TILE_Y = 4
WMAX = 8
DIRS = 2
GROUND = 512
TILES = 16384
N_ROW = 16


def draw_window(key, part):
    values = jax.random.randint(key, (DIRS,), 1, WMAX + 1, dtype=jnp.int32)
    chosen_spot = jax.random.randint(jax.random.fold_in(key, 7), (), 0, DIRS, dtype=jnp.int32)
    return values.at[chosen_spot].set(WMAX)


def set_ends(result, rng, smallest, high):
    spot = [jax.random.randint(jax.random.fold_in(rng, axis), (), 0, length) for axis, length in enumerate(result.shape)]
    main_axis = result.shape.index(max(result.shape))
    beside = spot[:main_axis] + [(spot[main_axis] + 1) % result.shape[main_axis]] + spot[main_axis + 1:]
    return result.at[tuple(spot)].set(smallest).at[tuple(beside)].set(high)


def block_levels(stream_key, shape, split, smallest, largest):
    def one(axis_at, blocks):
        draws = jax.random.uniform(jax.random.fold_in(jax.random.fold_in(stream_key, 6), axis_at), (blocks,), jnp.float32, smallest / len(split), largest / len(split))
        return jnp.repeat(jnp.exp(draws), shape[axis_at] // blocks).reshape((-1,) + (1,) * (len(shape) - axis_at - 1))

    level = one(*split[0])
    for cut in split[1:]:
        level = level * one(*cut)
    return level


def noise(key, extent, scale, most, split=(), kind=jnp.bfloat16):
    factor_of = block_levels(key, extent, split, -0.22, 0.18) if split else 1.0
    values = jax.random.normal(key, extent, jnp.float32) * scale * factor_of
    return jnp.minimum(jnp.maximum(values, -most), most).astype(kind)


def setup_inputs(seed: int = 0) -> dict:
    keys = jax.random.split(jax.random.key(seed), 7)
    return {
        "white_noise": noise(keys[0], (2, N, N), 1.0, 6.0, ((1, 32),)),
        "geometry": set_ends(jax.random.randint(keys[1], (DIRS, 2), 0, 4), jax.random.fold_in(keys[1], 1), 0, 3).astype(jnp.int32),
        "window": draw_window(jax.random.fold_in(keys[6], 71), 0),
        "tile_map": set_ends(jax.random.randint(keys[3], (DIRS, GROUND), 0, TILES), jax.random.fold_in(keys[3], 1), 0, TILES - 1).astype(jnp.int32),
        "link_gain": jnp.clip(jnp.exp(math.log(1.0) - 2.3025851 * jax.random.uniform(keys[4], (DIRS, GROUND), jnp.float32) ** block_levels(keys[4], (DIRS, GROUND), ((0, 2),), -0.2, 0.2)), 0.1, 1.0),
        "serving": set_ends(jax.random.randint(keys[5], (GROUND,), 0, DIRS), jax.random.fold_in(keys[5], 1), 0, DIRS - 1).astype(jnp.int32),
    }


full_turn = 2.0 * math.pi
noise_floor = 0.05
tiny_value = 1e-6
strength = 1.6
row_patterns = ("zrab,zwak->wrkb", "zrkb,zwbc->wrkc", "zrkc,wzbc->wrkb", "zrkb,wzak->wrab", "zrkb,zak->rab")
column_patterns = ("zaby,zwak->wkby", "zkby,zwbc->wkcy", "zkcy,wzbc->wkby", "zkby,wzak->waby", "zkby,zak->aby")


def complex_block(real_part, imag_part):
    return jnp.stack([jnp.stack([real_part, imag_part]), jnp.stack([-imag_part, real_part])]).astype(jnp.bfloat16)


def transform_tables(first, second):
    total = first * second
    outer_ids = jnp.arange(first, dtype=jnp.int32)
    inner_ids = jnp.arange(second, dtype=jnp.int32)
    outer_angle = ((outer_ids[:, None] * outer_ids[None, :]) % first).astype(jnp.float32) * (full_turn / first)
    inner_angle = ((inner_ids[:, None] * inner_ids[None, :]) % second).astype(jnp.float32) * (full_turn / second)
    twist_angle = ((outer_ids[:, None] * inner_ids[None, :]) % total).astype(jnp.float32) * (full_turn / total)
    return (complex_block(jnp.cos(outer_angle), -jnp.sin(outer_angle)),
            complex_block(jnp.cos(inner_angle), -jnp.sin(inner_angle)),
            jnp.cos(twist_angle), -jnp.sin(twist_angle))


def signed_wave(positions, first, second):
    total = first * second
    wave_number = positions // second + first * (positions % second)
    return jnp.where(wave_number >= total // 2, wave_number - total, wave_number).astype(jnp.float32)


def spectral_filter(row_ids, column_ids):
    wave_rows = signed_wave(row_ids, FIRST, SECOND)
    wave_columns = signed_wave(column_ids, FIRST, SECOND)
    squared_radius = 16.0 + wave_rows[:, None] ** 2 + wave_columns[None, :] ** 2
    return strength * float(N) * float(N) * squared_radius ** -0.75


def fresnel_factor(geometry_row, first, second):
    total = first * second
    fresnel_area = 144.0 * jnp.exp2(geometry_row[0].astype(jnp.float32))
    positions = jnp.arange(total, dtype=jnp.int32).reshape(first, second)
    scaled = signed_wave(positions, first, second) * (full_turn / total)
    turning = 0.5 * scaled * scaled * fresnel_area
    return jnp.cos(turning), -jnp.sin(turning)


def complex_times(values, real_part, imag_part):
    return jnp.stack([values[0] * real_part - values[1] * imag_part, values[0] * imag_part + values[1] * real_part])


def contract(pattern, operand, matrix):
    return jnp.einsum(pattern, operand.astype(jnp.float32), matrix.astype(jnp.float32))


def table_length(tables):
    return tables[0].shape[2] * tables[1].shape[2]


def forward_axis(values, tables, factor, patterns, trailing):
    outer_table, inner_table, twist_real, twist_imag = tables
    factor_real, factor_imag = factor
    if trailing:
        twist_real, twist_imag = twist_real[..., None], twist_imag[..., None]
        factor_real, factor_imag = factor_real[..., None], factor_imag[..., None]
    section_one = complex_times(contract(patterns[0], values, outer_table), twist_real, twist_imag).astype(jnp.bfloat16)
    section_two = contract(patterns[1], section_one, inner_table)
    return complex_times(section_two, factor_real, factor_imag).astype(jnp.bfloat16)


def inverse_first(values, tables, patterns, trailing):
    outer_table, inner_table, twist_real, twist_imag = tables
    if trailing:
        twist_real, twist_imag = twist_real[..., None], twist_imag[..., None]
    return complex_times(contract(patterns[2], values, inner_table), twist_real, -twist_imag).astype(jnp.bfloat16)


def inverse_axis(values, tables, patterns, trailing):
    section_one = inverse_first(values, tables, patterns, trailing)
    return contract(patterns[3], section_one, tables[0]) * (1.0 / table_length(tables))


def inverse_real(values, tables, patterns, trailing):
    section_one = inverse_first(values, tables, patterns, trailing)
    return contract(patterns[4], section_one, tables[0][0]) * (1.0 / table_length(tables))


def window_matrix(half_width):
    positions = jnp.arange(XTILES, dtype=jnp.int32)
    difference = (positions[:, None] - positions[None, :]) % XTILES
    distance = jnp.minimum(difference, XTILES - difference)
    return (distance <= half_width).astype(jnp.float32)


def tile_statistics(first_moment, second_moment, half_width, tile_rows):
    window_mask = window_matrix(half_width)
    cells = ((2 * half_width + 1) * (TILE_X * tile_rows)).astype(jnp.float32)
    mean_one = jnp.dot(first_moment, window_mask, precision=lax.Precision.HIGHEST) / cells
    mean_two = jnp.dot(second_moment, window_mask, precision=lax.Precision.HIGHEST) / cells
    fluctuation = mean_two / (mean_one * mean_one + tiny_value) - 1.0
    return fluctuation, mean_one * jnp.exp(-fluctuation)


def reference(white_noise, geometry, window, tile_map, link_gain, serving):
    tables_x = transform_tables(FIRST, SECOND)
    tables_y = transform_tables(N_ROW, ROWS_DEV)
    all_ids = jnp.arange(N, dtype=jnp.int32)
    spectrum = (white_noise.astype(jnp.float32) * spectral_filter(all_ids, all_ids)).astype(jnp.bfloat16)
    half_screen = inverse_axis(spectrum.reshape(2, N, FIRST, SECOND), tables_x, row_patterns, False)
    half_screen = half_screen.astype(jnp.bfloat16).reshape(2, N, N)
    phase_screen = inverse_real(half_screen.reshape(2, FIRST, SECOND, N), tables_x, column_patterns, True).reshape(N, N)

    def one_direction(inputs):
        geometry_row, half_width, tile_row, gain_row, direction = inputs
        slant_factor = 1.0 + 0.25 * geometry_row[1].astype(jnp.float32)
        fresnel_x = fresnel_factor(geometry_row, FIRST, SECOND)
        fresnel_y = fresnel_factor(geometry_row, N_ROW, ROWS_DEV)
        offset_rows = (N // 4) * geometry_row[1]
        patch_ids = ((offset_rows + jnp.arange(PATCH, dtype=jnp.int32)) % N).astype(jnp.int32)
        patch = jnp.take(phase_screen, patch_ids, axis=0)
        turned_phase = slant_factor * patch
        screen_field = jnp.stack([jnp.cos(turned_phase), jnp.sin(turned_phase)]).astype(jnp.bfloat16)
        spectral = forward_axis(screen_field.reshape(2, N_ROW, ROWS_DEV, N), tables_y, fresnel_y, column_patterns, True)
        first_pass = inverse_axis(spectral, tables_y, column_patterns, True).astype(jnp.bfloat16).reshape(2, PATCH, N)
        spectral = forward_axis(first_pass.reshape(2, PATCH, FIRST, SECOND), tables_x, fresnel_x, row_patterns, False)
        wave_field = inverse_axis(spectral, tables_x, row_patterns, False).reshape(2, PATCH, N)
        intensity = wave_field[0] * wave_field[0] + wave_field[1] * wave_field[1]
        intensity = intensity.reshape(YTILES * N_ROW, TILE_Y, XTILES, TILE_X)
        first_moment = jnp.sum(intensity, axis=(1, 3))
        second_moment = jnp.sum(intensity * intensity, axis=(1, 3))
        fluctuation, faded_power = tile_statistics(first_moment, second_moment, half_width, TILE_Y)
        received = gain_row * jnp.take(faded_power.reshape(-1), tile_row)
        serves_here = serving == direction
        return fluctuation, jnp.where(serves_here, received, 0.0), jnp.where(serves_here, 0.0, received)

    direction_ids = jnp.arange(DIRS, dtype=jnp.int32)
    fluctuation, signal_parts, interference_parts = lax.map(
        one_direction, (geometry, window, tile_map, link_gain, direction_ids))
    signal = jnp.sum(signal_parts, axis=0)
    interference = jnp.sum(interference_parts, axis=0)
    signal_ratio = jnp.log10(signal / (interference + noise_floor))
    return fluctuation, signal_ratio
```

```python
import math

import jax
import jax.numpy as jnp
from jax import lax
from jax.sharding import PartitionSpec as P

N = 8192
FIRST = 64
SECOND = 128
ROWS_DEV = 32
XTILES = 128
YTILES = 8
TILE_X = 64


full_turn = 2.0 * math.pi
noise_floor = 0.05
tiny_value = 1e-06
strength = 1.6
row_patterns = (
    "zrab,zwak->wrkb",
    "zrkb,zwbc->wrkc",
    "zrkc,wzbc->wrkb",
    "zrkb,wzak->wrab",
    "zrkb,zak->rab",
)
column_patterns = (
    "zaby,zwak->wkby",
    "zkby,zwbc->wkcy",
    "zkcy,wzbc->wkby",
    "zkby,wzak->waby",
    "zkby,zak->aby",
)


def complex_block(real_part, imag_part):
    return jnp.stack(
        [jnp.stack([real_part, imag_part]), jnp.stack([-imag_part, real_part])]
    ).astype(jnp.bfloat16)


def transform_tables(first, second):
    total = first * second
    outer_ids = jnp.arange(first, dtype=jnp.int32)
    inner_ids = jnp.arange(second, dtype=jnp.int32)
    outer_angle = (outer_ids[:, None] * outer_ids[None, :] % first).astype(jnp.float32) * (
        full_turn / first
    )
    inner_angle = (inner_ids[:, None] * inner_ids[None, :] % second).astype(jnp.float32) * (
        full_turn / second
    )
    twist_angle = (outer_ids[:, None] * inner_ids[None, :] % total).astype(jnp.float32) * (
        full_turn / total
    )
    return (
        complex_block(jnp.cos(outer_angle), -jnp.sin(outer_angle)),
        complex_block(jnp.cos(inner_angle), -jnp.sin(inner_angle)),
        jnp.cos(twist_angle),
        -jnp.sin(twist_angle),
    )


def signed_wave(positions, first, second):
    total = first * second
    wave_number = positions // second + first * (positions % second)
    return jnp.where(wave_number >= total // 2, wave_number - total, wave_number).astype(
        jnp.float32
    )


def spectral_filter(row_ids, column_ids):
    wave_rows = signed_wave(row_ids, FIRST, SECOND)
    wave_columns = signed_wave(column_ids, FIRST, SECOND)
    squared_radius = 16.0 + wave_rows[:, None] ** 2 + wave_columns[None, :] ** 2
    return strength * float(N) * float(N) * squared_radius ** (-0.75)


def fresnel_factor(geometry_row, first, second):
    total = first * second
    fresnel_area = 144.0 * jnp.exp2(geometry_row[0].astype(jnp.float32))
    positions = jnp.arange(total, dtype=jnp.int32).reshape(first, second)
    scaled = signed_wave(positions, first, second) * (full_turn / total)
    turning = 0.5 * scaled * scaled * fresnel_area
    return (jnp.cos(turning), -jnp.sin(turning))


def complex_times(values, real_part, imag_part):
    return jnp.stack(
        [
            values[0] * real_part - values[1] * imag_part,
            values[0] * imag_part + values[1] * real_part,
        ]
    )


def contract(pattern, operand, matrix):
    return jnp.einsum(pattern, operand, matrix, preferred_element_type=jnp.float32)


def table_length(tables):
    return tables[0].shape[2] * tables[1].shape[2]


def forward_axis(values, tables, factor, patterns, trailing):
    outer_table, inner_table, twist_real, twist_imag = tables
    factor_real, factor_imag = factor
    if trailing:
        twist_real, twist_imag = (twist_real[..., None], twist_imag[..., None])
        factor_real, factor_imag = (factor_real[..., None], factor_imag[..., None])
    section_one = complex_times(
        contract(patterns[0], values, outer_table), twist_real, twist_imag
    ).astype(jnp.bfloat16)
    section_two = contract(patterns[1], section_one, inner_table)
    return complex_times(section_two, factor_real, factor_imag).astype(jnp.bfloat16)


def inverse_first(values, tables, patterns, trailing):
    outer_table, inner_table, twist_real, twist_imag = tables
    if trailing:
        twist_real, twist_imag = (twist_real[..., None], twist_imag[..., None])
    return complex_times(
        contract(patterns[2], values, inner_table), twist_real, -twist_imag
    ).astype(jnp.bfloat16)


def inverse_axis(values, tables, patterns, trailing):
    section_one = inverse_first(values, tables, patterns, trailing)
    return contract(patterns[3], section_one, tables[0]) * (1.0 / table_length(tables))


def window_matrix(half_width):
    positions = jnp.arange(XTILES, dtype=jnp.int32)
    difference = (positions[:, None] - positions[None, :]) % XTILES
    distance = jnp.minimum(difference, XTILES - difference)
    return (distance <= half_width).astype(jnp.float32)


def tile_statistics(first_moment, second_moment, half_width, tile_rows):
    window_mask = window_matrix(half_width)
    cells = ((2 * half_width + 1) * (TILE_X * tile_rows)).astype(jnp.float32)
    mean_one = jnp.dot(first_moment, window_mask, precision=lax.Precision.HIGHEST) / cells
    mean_two = jnp.dot(second_moment, window_mask, precision=lax.Precision.HIGHEST) / cells
    fluctuation = mean_two / (mean_one * mean_one + tiny_value) - 1.0
    return (fluctuation, mean_one * jnp.exp(-fluctuation))


def propagate_columns(phase_patch, tables_y, slant_factor, fresnel_y):
    patch_rows = phase_patch.shape[0]
    width_here = phase_patch.shape[1]
    outer_len = tables_y[0].shape[2]
    inner_len = tables_y[1].shape[2]
    turned_phase = slant_factor * phase_patch
    screen_field = jnp.stack([jnp.cos(turned_phase), jnp.sin(turned_phase)]).astype(jnp.bfloat16)
    stacked = screen_field.reshape(2, outer_len, inner_len, width_here)
    spectral = forward_axis(stacked, tables_y, fresnel_y, column_patterns, True)
    result = inverse_axis(spectral, tables_y, column_patterns, True)
    return result.astype(jnp.bfloat16).reshape(2, patch_rows, width_here)


def gathered_patch(half_screen, geometry, tables, patch_len):
    turned = lax.all_to_all(half_screen, "row", split_axis=2, concat_axis=1, tiled=True)
    band_rows = turned.shape[1]
    columns = turned.shape[2]
    offset_rows = N // 4 * geometry[0, 1]
    blocks = band_rows // SECOND
    block_start = lax.axis_index("dir") * blocks
    stacked = turned.reshape(2, blocks, SECOND, columns)
    twist_real = lax.dynamic_slice_in_dim(tables[2], block_start, blocks, 0)[..., None]
    twist_imag = lax.dynamic_slice_in_dim(tables[3], block_start, blocks, 0)[..., None]
    section_one = complex_times(
        contract("zkcx,wzbc->wkbx", stacked, tables[1]), twist_real, -twist_imag
    )
    section_one = section_one.astype(jnp.bfloat16)
    outer_count = patch_len // SECOND
    outer_ids = (offset_rows // SECOND + jnp.arange(outer_count, dtype=jnp.int32)) % FIRST
    patch_outer = jnp.take(tables[0][0], outer_ids, axis=1)
    phase_patch = contract(
        "zkbx,zak->abx", lax.all_gather(section_one, "dir", axis=1, tiled=True), patch_outer
    )
    return phase_patch.reshape(patch_len, columns) * (1.0 / N)


def patch_matrix(slant_bin, block_ids, outer_count):
    inner_ids = jnp.arange(SECOND, dtype=jnp.int32)
    outer_ids = slant_bin * (FIRST // 4) + jnp.arange(outer_count, dtype=jnp.int32)
    whole_position = outer_ids[:, None] * SECOND + inner_ids[None, :]
    slow = (whole_position[:, :, None] * block_ids[None, None, :] % N).astype(jnp.float32) * (
        full_turn / N
    )
    fast = (inner_ids[:, None] * inner_ids[None, :] % SECOND).astype(jnp.float32) * (
        full_turn / SECOND
    )
    slow_real, slow_imag = (jnp.cos(slow)[..., None], jnp.sin(slow)[..., None])
    fast_real, fast_imag = (jnp.cos(fast)[None, :, None, :], jnp.sin(fast)[None, :, None, :])
    real_part = slow_real * fast_real - slow_imag * fast_imag
    imag_part = slow_real * fast_imag + slow_imag * fast_real
    pairs = [part.reshape(outer_count, SECOND, 2, 2, SECOND) for part in (real_part, -imag_part)]
    matrix = jnp.stack(pairs, axis=3).astype(jnp.bfloat16)
    return matrix.reshape(outer_count * SECOND, 8 * SECOND)


def reduced_patch(half_screen, geometry):
    row_count = lax.axis_size("row")
    patch_len = row_count * ROWS_DEV
    outer_count = patch_len // SECOND
    row = lax.axis_index("row")
    core, y_spot = (row % 2, row // 2 % 2)
    over_core = [(r, r ^ 1) for r in range(row_count)]
    over_y = [(r, r ^ 2) for r in range(row_count)]
    over_x = [(0, 1), (1, 0)]
    z_groups = [[r + 4 * z for z in range(4)] for r in range(4)]
    other_bin = lax.ppermute(geometry[0, 1], "dir", over_x)
    spread = half_screen.reshape(2 * half_screen.shape[1], 4, 2, 2, 512)
    kept = lax.dynamic_index_in_dim(spread, core, 3, keepdims=False)
    moved = lax.dynamic_index_in_dim(spread, 1 - core, 3, keepdims=False)
    joined = jnp.concatenate([kept, lax.ppermute(moved, "row", over_core)], axis=0)
    first_block = 2 * (lax.axis_index("dir") * row_count + row)
    other_block = 2 * (lax.axis_index("dir") * row_count + (row ^ 1))
    block_ids = jnp.stack([first_block, first_block + 1, other_block, other_block + 1])
    own = patch_matrix(geometry[0, 1], block_ids, outer_count)
    other = patch_matrix(other_bin, block_ids, outer_count)
    y_kept = lax.dynamic_index_in_dim(joined, y_spot, 2, keepdims=False)
    y_moved = lax.dynamic_index_in_dim(joined, 1 - y_spot, 2, keepdims=False)
    halves = [
        (y_kept[:, :, :256], y_moved[:, :, :256]),
        (y_kept[:, :, 256:], y_moved[:, :, 256:]),
    ]

    def partial(matrix, values):
        return contract("nk,kzx->nzx", matrix, values)

    def narrow(values):
        return values.astype(jnp.bfloat16)

    (a_kept, a_moved), (b_kept, b_moved) = halves
    a_recv_kept = lax.ppermute(narrow(partial(other, a_kept)), "dir", over_x)
    a_recv_moved = lax.ppermute(narrow(partial(other, a_moved)), "dir", over_x)
    b_recv_other = lax.ppermute(narrow(partial(other, b_moved)), "row", over_y)
    b_recv_own = lax.ppermute(narrow(partial(own, b_moved)), "row", over_y)
    a_second = lax.ppermute(narrow(partial(own, a_moved) + a_recv_moved), "row", over_y)
    b_second = lax.ppermute(narrow(partial(other, b_kept) + b_recv_other), "dir", over_x)
    a_total = narrow(partial(own, a_kept) + a_recv_kept + a_second)
    b_total = narrow(partial(own, b_kept) + b_recv_own + b_second)
    total = jnp.concatenate([a_total, b_total], axis=2)
    pieces = lax.all_to_all(
        total, "row", split_axis=1, concat_axis=1, axis_index_groups=z_groups, tiled=True
    )
    return jnp.sum(pieces.astype(jnp.float32), axis=1) * (1.0 / N)


def body(white_noise, geometry, window, tile_map, link_gain, serving):
    row_count = lax.axis_size("row")
    tables = transform_tables(FIRST, SECOND)
    tables_y = transform_tables(row_count, ROWS_DEV)
    patch_len = row_count * ROWS_DEV
    rows_here = white_noise.shape[1]
    row_start = lax.axis_index(("dir", "row")) * rows_here
    row_ids = row_start + jnp.arange(rows_here, dtype=jnp.int32)
    column_ids = jnp.arange(N, dtype=jnp.int32)
    spectral_gain = spectral_filter(row_ids, column_ids)
    spectrum = (white_noise.astype(jnp.float32) * spectral_gain).astype(jnp.bfloat16)
    half_screen = inverse_axis(
        spectrum.reshape(2, rows_here, FIRST, SECOND), tables, row_patterns, False
    )
    half_screen = half_screen.astype(jnp.bfloat16).reshape(2, rows_here, N)
    slant_factor = 1.0 + 0.25 * geometry[0, 1].astype(jnp.float32)
    fresnel_x = fresnel_factor(geometry[0], FIRST, SECOND)
    fresnel_y = fresnel_factor(geometry[0], row_count, ROWS_DEV)
    if lax.axis_size("dir") == 2 and row_count == 16 and rows_here % SECOND == 0:
        phase_patch = reduced_patch(half_screen, geometry)
    else:
        phase_patch = gathered_patch(half_screen, geometry, tables, patch_len)
    columns = phase_patch.shape[1]
    screen_field = propagate_columns(phase_patch, tables_y, slant_factor, fresnel_y)
    stacked_field = screen_field.reshape(2, row_count, ROWS_DEV, columns)
    portion = lax.all_to_all(stacked_field, "row", split_axis=1, concat_axis=3, tiled=True)
    item_count = portion.shape[2]
    stacked = portion.reshape(2, item_count, FIRST, SECOND)
    spectral = forward_axis(stacked, tables, fresnel_x, row_patterns, False)
    wave_field = inverse_axis(spectral, tables, row_patterns, False)
    intensity = wave_field[0] * wave_field[0] + wave_field[1] * wave_field[1]
    intensity = intensity.reshape(item_count, XTILES, TILE_X)
    tile_one = jnp.sum(intensity, axis=2)
    tile_two = jnp.sum(intensity * intensity, axis=2)
    tile_rows = ROWS_DEV // YTILES
    first_moment = jnp.sum(tile_one.reshape(YTILES, tile_rows, XTILES), axis=1)
    second_moment = jnp.sum(tile_two.reshape(YTILES, tile_rows, XTILES), axis=1)
    fluctuation, faded_power = tile_statistics(first_moment, second_moment, window[0], tile_rows)
    faded_flat = faded_power.reshape(-1)
    tile_total = faded_flat.shape[0]
    local_tile = tile_map[0] - lax.axis_index("row") * tile_total
    inside = (local_tile >= 0) & (local_tile < tile_total)
    looked = jnp.where(inside, jnp.take(faded_flat, jnp.clip(local_tile, 0, tile_total - 1)), 0.0)
    received = link_gain[0] * looked
    direction = lax.axis_index("dir")
    serves_here = serving == direction
    signal_part = jnp.where(serves_here, received, 0.0)
    interference_part = jnp.where(serves_here, 0.0, received)
    device_count = lax.axis_size(("dir", "row"))
    terms = jnp.stack([signal_part, interference_part]).reshape(2, device_count, -1)
    gathered = lax.all_to_all(
        terms.transpose(1, 0, 2), ("dir", "row"), split_axis=0, concat_axis=0, tiled=True
    )
    signal, interference = jnp.sum(gathered, axis=0)
    signal_ratio = jnp.log10(signal / (interference + noise_floor))
    return (fluctuation[None], signal_ratio)


def solution(mesh):
    return jax.shard_map(
        body,
        mesh=mesh,
        in_specs=(
            P(None, ("dir", "row"), None),
            P("dir", None),
            P("dir"),
            P("dir", None),
            P("dir", None),
            P(),
        ),
        out_specs=(P("dir", "row", None), P(("dir", "row"))),
        check_vma=False,
    )
```

```python
import math

import jax
import jax.numpy as jnp
import ml_dtypes
import numpy as np
from jax import lax
from jax.experimental import pallas as pl
from jax.experimental.pallas import tpu as pltpu
from jax.sharding import PartitionSpec as P

N = 8192
FIRST = 64
SECOND = 128
ROWS_DEV = 32
XTILES = 128
YTILES = 8
TILE_X = 64
GROUP = 8
CHUNKS = 4


full_turn = 2.0 * math.pi
noise_floor = 0.05
tiny_value = 1e-06
strength = 1.6
row_patterns = (
    "zrab,zwak->wrkb",
    "zrkb,zwbc->wrkc",
    "zrkc,wzbc->wrkb",
    "zrkb,wzak->wrab",
    "zrkb,zak->rab",
)
column_patterns = (
    "zaby,zwak->wkby",
    "zkby,zwbc->wkcy",
    "zkcy,wzbc->wkby",
    "zkby,wzak->waby",
    "zkby,zak->aby",
)


def complex_block(real_part, imag_part):
    return jnp.stack(
        [jnp.stack([real_part, imag_part]), jnp.stack([-imag_part, real_part])]
    ).astype(jnp.bfloat16)


def transform_tables(first, second):
    total = first * second
    outer_ids = jnp.arange(first, dtype=jnp.int32)
    inner_ids = jnp.arange(second, dtype=jnp.int32)
    outer_angle = (outer_ids[:, None] * outer_ids[None, :] % first).astype(jnp.float32) * (
        full_turn / first
    )
    inner_angle = (inner_ids[:, None] * inner_ids[None, :] % second).astype(jnp.float32) * (
        full_turn / second
    )
    twist_angle = (outer_ids[:, None] * inner_ids[None, :] % total).astype(jnp.float32) * (
        full_turn / total
    )
    return (
        complex_block(jnp.cos(outer_angle), -jnp.sin(outer_angle)),
        complex_block(jnp.cos(inner_angle), -jnp.sin(inner_angle)),
        jnp.cos(twist_angle),
        -jnp.sin(twist_angle),
    )


def signed_wave(positions, first, second):
    total = first * second
    wave_number = positions // second + first * (positions % second)
    return jnp.where(wave_number >= total // 2, wave_number - total, wave_number).astype(
        jnp.float32
    )


def spectral_filter(row_ids, column_ids):
    wave_rows = signed_wave(row_ids, FIRST, SECOND)
    wave_columns = signed_wave(column_ids, FIRST, SECOND)
    squared_radius = 16.0 + wave_rows[:, None] ** 2 + wave_columns[None, :] ** 2
    return strength * float(N) * float(N) * squared_radius ** (-0.75)


def fresnel_factor(geometry_row, first, second):
    total = first * second
    fresnel_area = 144.0 * jnp.exp2(geometry_row[0].astype(jnp.float32))
    positions = jnp.arange(total, dtype=jnp.int32).reshape(first, second)
    scaled = signed_wave(positions, first, second) * (full_turn / total)
    turning = 0.5 * scaled * scaled * fresnel_area
    return (jnp.cos(turning), -jnp.sin(turning))


def complex_times(values, real_part, imag_part):
    return jnp.stack(
        [
            values[0] * real_part - values[1] * imag_part,
            values[0] * imag_part + values[1] * real_part,
        ]
    )


def contract(pattern, operand, matrix):
    return jnp.einsum(pattern, operand, matrix, preferred_element_type=jnp.float32)


def table_length(tables):
    return tables[0].shape[2] * tables[1].shape[2]


def forward_axis(values, tables, factor, patterns, trailing):
    outer_table, inner_table, twist_real, twist_imag = tables
    factor_real, factor_imag = factor
    if trailing:
        twist_real, twist_imag = (twist_real[..., None], twist_imag[..., None])
        factor_real, factor_imag = (factor_real[..., None], factor_imag[..., None])
    section_one = complex_times(
        contract(patterns[0], values, outer_table), twist_real, twist_imag
    ).astype(jnp.bfloat16)
    section_two = contract(patterns[1], section_one, inner_table)
    return complex_times(section_two, factor_real, factor_imag).astype(jnp.bfloat16)


def inverse_first(values, tables, patterns, trailing):
    outer_table, inner_table, twist_real, twist_imag = tables
    if trailing:
        twist_real, twist_imag = (twist_real[..., None], twist_imag[..., None])
    return complex_times(
        contract(patterns[2], values, inner_table), twist_real, -twist_imag
    ).astype(jnp.bfloat16)


def inverse_axis(values, tables, patterns, trailing):
    section_one = inverse_first(values, tables, patterns, trailing)
    return contract(patterns[3], section_one, tables[0]) * (1.0 / table_length(tables))


def window_matrix(half_width):
    positions = jnp.arange(XTILES, dtype=jnp.int32)
    difference = (positions[:, None] - positions[None, :]) % XTILES
    distance = jnp.minimum(difference, XTILES - difference)
    return (distance <= half_width).astype(jnp.float32)


def tile_statistics(first_moment, second_moment, half_width, tile_rows):
    window_mask = window_matrix(half_width)
    cells = ((2 * half_width + 1) * (TILE_X * tile_rows)).astype(jnp.float32)
    mean_one = jnp.dot(first_moment, window_mask, precision=lax.Precision.HIGHEST) / cells
    mean_two = jnp.dot(second_moment, window_mask, precision=lax.Precision.HIGHEST) / cells
    fluctuation = mean_two / (mean_one * mean_one + tiny_value) - 1.0
    return (fluctuation, mean_one * jnp.exp(-fluctuation))


def propagate_columns(phase_patch, tables_y, slant_factor, fresnel_y):
    patch_rows = phase_patch.shape[0]
    width_here = phase_patch.shape[1]
    outer_len = tables_y[0].shape[2]
    inner_len = tables_y[1].shape[2]
    turned_phase = slant_factor * phase_patch
    screen_field = jnp.stack([jnp.cos(turned_phase), jnp.sin(turned_phase)]).astype(jnp.bfloat16)
    stacked = screen_field.reshape(2, outer_len, inner_len, width_here)
    spectral = forward_axis(stacked, tables_y, fresnel_y, column_patterns, True)
    result = inverse_axis(spectral, tables_y, column_patterns, True)
    return result.astype(jnp.bfloat16).reshape(2, patch_rows, width_here)


def half_screen_rows(white_noise, row_start, tables):
    rows_here = white_noise.shape[1]
    row_ids = row_start + jnp.arange(rows_here, dtype=jnp.int32)
    column_ids = jnp.arange(N, dtype=jnp.int32)
    spectral_gain = spectral_filter(row_ids, column_ids)
    spectrum = (white_noise.astype(jnp.float32) * spectral_gain).astype(jnp.bfloat16)
    half_screen = inverse_axis(
        spectrum.reshape(2, rows_here, FIRST, SECOND), tables, row_patterns, False
    )
    half_screen = half_screen.astype(jnp.bfloat16).reshape(2, rows_here, N)
    return half_screen


def gathered_patch(half_screen, geometry, tables, patch_len):
    turned = lax.all_to_all(half_screen, "row", split_axis=2, concat_axis=1, tiled=True)
    band_rows = turned.shape[1]
    columns = turned.shape[2]
    offset_rows = N // 4 * geometry[0, 1]
    blocks = band_rows // SECOND
    block_start = lax.axis_index("dir") * blocks
    stacked = turned.reshape(2, blocks, SECOND, columns)
    twist_real = lax.dynamic_slice_in_dim(tables[2], block_start, blocks, 0)[..., None]
    twist_imag = lax.dynamic_slice_in_dim(tables[3], block_start, blocks, 0)[..., None]
    section_one = complex_times(
        contract("zkcx,wzbc->wkbx", stacked, tables[1]), twist_real, -twist_imag
    )
    section_one = section_one.astype(jnp.bfloat16)
    outer_count = patch_len // SECOND
    outer_ids = (offset_rows // SECOND + jnp.arange(outer_count, dtype=jnp.int32)) % FIRST
    patch_outer = jnp.take(tables[0][0], outer_ids, axis=1)
    phase_patch = contract(
        "zkbx,zak->abx", lax.all_gather(section_one, "dir", axis=1, tiled=True), patch_outer
    )
    return phase_patch.reshape(patch_len, columns) * (1.0 / N)


def host_tables():
    def block(length):
        ids = np.arange(length)
        angle = (ids[:, None] * ids[None, :] % length) * (full_turn / length)
        real_part, imag_part = (np.cos(angle), np.sin(angle))
        return np.array([[real_part, -imag_part], [imag_part, real_part]])

    inner = block(SECOND).transpose(1, 3, 0, 2).reshape(2 * SECOND, 2 * SECOND)
    outer = block(FIRST).transpose(0, 2, 1, 3).reshape(2 * FIRST, 2 * FIRST)
    spread = np.kron(outer, np.eye(GROUP))
    twist = np.arange(FIRST)[:, None] * np.arange(SECOND)[None, :] * (full_turn / N)
    twist = np.repeat(twist, GROUP, axis=0)
    angle = (np.arange(SECOND)[:, None] * np.arange(SECOND)[None, :] % SECOND) * (full_turn / SECOND)
    return (
        inner.astype(ml_dtypes.bfloat16),
        np.stack([np.cos(twist), np.sin(twist)]).astype(np.float32),
        spread.astype(ml_dtypes.bfloat16),
        np.stack([np.cos(angle), np.sin(angle)]).astype(np.float32),
    )


def screen_kernel(
    spot, noise, rows_squared, columns_squared, inner, twist, spread, kept, moved, staged
):
    core, y_spot = (spot[0], spot[1])
    root = lax.rsqrt(16.0 + rows_squared[...] + columns_squared[...])
    gain = strength * root * (root * lax.rsqrt(root))
    spectrum = [noise[z].astype(jnp.float32) * gain for z in range(2)]
    sections = []
    for group in range(2):
        rows = slice(group * GROUP, (group + 1) * GROUP)
        parts = [
            jnp.concatenate(
                [spectrum[z][rows, k * SECOND : (k + 1) * SECOND] for k in range(FIRST)], axis=0
            ).astype(jnp.bfloat16)
            for z in range(2)
        ]
        first = jnp.dot(
            jnp.concatenate(parts, axis=1), inner[...], preferred_element_type=jnp.float32
        )
        real_part, imag_part = (first[:, :SECOND], first[:, SECOND:])
        turned = jnp.concatenate(
            [
                real_part * twist[0] - imag_part * twist[1],
                real_part * twist[1] + imag_part * twist[0],
            ],
            axis=0,
        )
        sections.append(turned.astype(jnp.bfloat16))
    staged[...] = jnp.dot(
        spread[...], jnp.concatenate(sections, axis=1), preferred_element_type=jnp.float32
    )
    for core_side, target in enumerate((kept, moved)):
        for y_side in range(2):
            for chunk in range(CHUNKS):
                for z_spot in range(4):
                    place = z_spot * 4 + (y_spot ^ y_side) * 2 + (core ^ core_side)
                    for w in range(2):
                        start = (w * FIRST + place * CHUNKS + chunk) * GROUP
                        taken = staged[pl.ds(pl.multiple_of(start, GROUP), GROUP), :]
                        both = jnp.concatenate([taken[:, :SECOND], taken[:, SECOND:]], axis=0)
                        target[y_side, chunk, w, :, z_spot * SECOND : (z_spot + 1) * SECOND] = (
                            both.astype(jnp.bfloat16)
                        )


def half_screens(white_noise, row_start, row, host):
    rows_here = white_noise.shape[1]
    inner, twist, spread, _ = host
    row_waves = signed_wave(row_start + jnp.arange(rows_here, dtype=jnp.int32), FIRST, SECOND)
    column_waves = signed_wave(jnp.arange(N, dtype=jnp.int32), FIRST, SECOND)
    spot = jnp.stack([row % 2, row // 2 % 2])
    step = 2 * GROUP
    out_shape = (2, CHUNKS, 2, rows_here, 4 * SECOND)
    out_spec = pl.BlockSpec((2, CHUNKS, 2, step, 4 * SECOND), lambda i: (0, 0, 0, i, 0))

    def whole(array):
        return pl.BlockSpec(array.shape, lambda i: (0,) * array.ndim)

    return pl.pallas_call(
        screen_kernel,
        grid=(rows_here // step,),
        in_specs=[
            pl.BlockSpec(memory_space=pltpu.SMEM),
            pl.BlockSpec((2, step, N), lambda i: (0, i, 0)),
            pl.BlockSpec((step, 1), lambda i: (i, 0)),
            pl.BlockSpec((1, N), lambda i: (0, 0)),
            whole(inner),
            whole(twist),
            whole(spread),
        ],
        out_specs=[out_spec, out_spec],
        out_shape=[jax.ShapeDtypeStruct(out_shape, jnp.bfloat16)] * 2,
        scratch_shapes=[pltpu.VMEM((2 * FIRST * GROUP, 2 * SECOND), jnp.float32)],
        compiler_params=pltpu.CompilerParams(vmem_limit_bytes=48 * 1024 * 1024),
        cost_estimate=pl.CostEstimate(
            flops=20_000_000_000, bytes_accessed=20_000_000, transcendentals=4_000_000
        ),
    )(
        spot,
        white_noise,
        (row_waves * row_waves)[:, None],
        (column_waves * column_waves)[None, :],
        inner,
        twist,
        spread,
    )


def matrix_kernel(slow, fast, matrix):
    for source in range(2):
        for near in range(2):
            block = source * 2 + near
            slow_real = slow[0, :, block : block + 1]
            slow_imag = slow[1, :, block : block + 1]
            real_part = slow_real * fast[0] - slow_imag * fast[1]
            imag_part = slow_real * fast[1] + slow_imag * fast[0]
            for z, part in enumerate((real_part, -imag_part)):
                start = ((source * 2 + z) * 2 + near) * SECOND
                matrix[:, start : start + SECOND] = part.astype(jnp.bfloat16)


def patch_matrix(slant_bins, block_ids, outer_count, fast):
    inner_ids = jnp.arange(SECOND, dtype=jnp.int32)
    outer_ids = slant_bins[:, None] * (FIRST // 4) + jnp.arange(outer_count, dtype=jnp.int32)
    position = (outer_ids[:, :, None] * SECOND + inner_ids).reshape(-1)
    slow = (position[:, None] * block_ids[None, :] % N).astype(jnp.float32) * (full_turn / N)
    slow = jnp.stack([jnp.cos(slow), jnp.sin(slow)])
    length = position.shape[0]
    return pl.pallas_call(
        matrix_kernel,
        grid=(length // SECOND,),
        in_specs=[
            pl.BlockSpec((2, SECOND, 4), lambda i: (0, i, 0)),
            pl.BlockSpec(fast.shape, lambda i: (0, 0, 0)),
        ],
        out_specs=pl.BlockSpec((SECOND, 8 * SECOND), lambda i: (i, 0)),
        out_shape=jax.ShapeDtypeStruct((length, 8 * SECOND), jnp.bfloat16),
        cost_estimate=pl.CostEstimate(
            flops=8_000_000, bytes_accessed=4_000_000, transcendentals=0
        ),
    )(slow, fast)


def product_kernel(matrix, kept, received, *rest):
    *added, result = rest
    depth = kept.shape[0] * kept.shape[1]
    total = jnp.dot(
        matrix[:, :depth],
        kept[...].reshape(depth, kept.shape[2]),
        preferred_element_type=jnp.float32,
    )
    total += jnp.dot(
        matrix[:, depth:],
        received[...].reshape(depth, kept.shape[2]),
        preferred_element_type=jnp.float32,
    )
    for term in added:
        total += term[...].astype(jnp.float32)
    result[...] = total.astype(result.dtype)


def patch_product(matrix, bins, kept, received, sides, chunk, *added):
    patch_len = matrix.shape[0] // 2
    _, _, parts, rows, columns = kept.shape
    bin_start, bin_count = bins
    side_start, side_count = sides
    values_spec = pl.BlockSpec(
        (None, None, parts, rows, columns), lambda i, j: (side_start + j, chunk, 0, 0, 0)
    )
    result_spec = pl.BlockSpec(
        (None, patch_len, columns), lambda i, j: (i * side_count + j, 0, 0)
    )
    count = bin_count * side_count
    return pl.pallas_call(
        product_kernel,
        grid=(bin_count, side_count),
        in_specs=[
            pl.BlockSpec((patch_len, matrix.shape[1]), lambda i, j: (bin_start + i, 0)),
            values_spec,
            values_spec,
        ]
        + [result_spec] * len(added),
        out_specs=result_spec,
        out_shape=jax.ShapeDtypeStruct((count, patch_len, columns), jnp.bfloat16),
        compiler_params=pltpu.CompilerParams(vmem_limit_bytes=32 * 1024 * 1024),
        cost_estimate=pl.CostEstimate(
            flops=2 * count * patch_len * matrix.shape[1] * columns,
            bytes_accessed=4_000_000,
            transcendentals=0,
        ),
    )(matrix, kept, received, *added)


def reduced_patch(white_noise, row_start, geometry):
    row_count = lax.axis_size("row")
    patch_len = row_count * ROWS_DEV
    row = lax.axis_index("row")
    z_spot = row // 4
    over_core = [(r, r ^ 1) for r in range(row_count)]
    over_y = [(r, r ^ 2) for r in range(row_count)]
    over_x = [(0, 1), (1, 0)]
    host = host_tables()
    other_bin = lax.ppermute(geometry[0, 1], "dir", over_x)
    kept, moved = half_screens(white_noise, row_start, row, host)
    received = lax.ppermute(moved, "row", over_core)
    first_block = 2 * (lax.axis_index("dir") * row_count + row)
    other_block = 2 * (lax.axis_index("dir") * row_count + (row ^ 1))
    block_ids = jnp.stack([first_block, first_block + 1, other_block, other_block + 1])
    slant_bins = jnp.stack([geometry[0, 1], other_bin])
    matrix = patch_matrix(slant_bins, block_ids, patch_len // SECOND, host[3])
    own, other, both = ((0, 1), (1, 1), (0, 2))

    def product(bins, sides, chunk, *added):
        return patch_product(matrix, bins, kept, received, sides, chunk, *added)

    def over(first_x, values):
        if first_x:
            return lax.ppermute(values, "dir", over_x)
        return lax.ppermute(values, "row", over_y)

    arrived = {}
    for chunk in range(CHUNKS):
        first_x = chunk % 2 == 0
        leaving = product(other, both, chunk) if first_x else product(both, other, chunk)
        if chunk >= 2:
            leaving, _ = lax.optimization_barrier((leaving, arrived[chunk - 2]))
        arrived[chunk] = over(first_x, leaving)
    totals = []
    for chunk in range(CHUNKS):
        first_x = chunk % 2 == 0
        first_kept, first_moved = (arrived[chunk][:1], arrived[chunk][1:])
        if first_x:
            second = product(own, other, chunk, first_moved)
        else:
            second = product(other, own, chunk, first_moved)
        second = over(not first_x, second)
        total = product(own, own, chunk, first_kept, second)[0]

        def slice_for(spot):
            return lax.dynamic_slice_in_dim(total, spot * SECOND, SECOND, 1)

        result = slice_for(z_spot).astype(jnp.float32)
        for shift in range(1, 4):
            pairs = [(r, r ^ (4 * shift)) for r in range(row_count)]
            sent = lax.ppermute(slice_for(z_spot ^ shift), "row", pairs)
            result = result + sent.astype(jnp.float32)
        totals.append(result)
    return jnp.concatenate(totals, axis=1)


def body(white_noise, geometry, window, tile_map, link_gain, serving):
    row_count = lax.axis_size("row")
    tables = transform_tables(FIRST, SECOND)
    tables_y = transform_tables(row_count, ROWS_DEV)
    patch_len = row_count * ROWS_DEV
    rows_here = white_noise.shape[1]
    row_start = lax.axis_index(("dir", "row")) * rows_here
    slant_factor = 1.0 + 0.25 * geometry[0, 1].astype(jnp.float32)
    fresnel_x = fresnel_factor(geometry[0], FIRST, SECOND)
    fresnel_y = fresnel_factor(geometry[0], row_count, ROWS_DEV)
    if lax.axis_size("dir") == 2 and row_count == 16 and rows_here == 2 * SECOND:
        phase_patch = reduced_patch(white_noise, row_start, geometry)
    else:
        half_screen = half_screen_rows(white_noise, row_start, tables)
        phase_patch = gathered_patch(half_screen, geometry, tables, patch_len)
    columns = phase_patch.shape[1]
    screen_field = propagate_columns(phase_patch, tables_y, slant_factor, fresnel_y)
    stacked_field = screen_field.reshape(2, row_count, ROWS_DEV, columns)
    portion = lax.all_to_all(stacked_field, "row", split_axis=1, concat_axis=3, tiled=True)
    item_count = portion.shape[2]
    stacked = portion.reshape(2, item_count, FIRST, SECOND)
    spectral = forward_axis(stacked, tables, fresnel_x, row_patterns, False)
    wave_field = inverse_axis(spectral, tables, row_patterns, False)
    intensity = wave_field[0] * wave_field[0] + wave_field[1] * wave_field[1]
    intensity = intensity.reshape(item_count, XTILES, TILE_X)
    tile_one = jnp.sum(intensity, axis=2)
    tile_two = jnp.sum(intensity * intensity, axis=2)
    tile_rows = ROWS_DEV // YTILES
    first_moment = jnp.sum(tile_one.reshape(YTILES, tile_rows, XTILES), axis=1)
    second_moment = jnp.sum(tile_two.reshape(YTILES, tile_rows, XTILES), axis=1)
    fluctuation, faded_power = tile_statistics(first_moment, second_moment, window[0], tile_rows)
    faded_flat = faded_power.reshape(-1)
    tile_total = faded_flat.shape[0]
    local_tile = tile_map[0] - lax.axis_index("row") * tile_total
    inside = (local_tile >= 0) & (local_tile < tile_total)
    looked = jnp.where(inside, jnp.take(faded_flat, jnp.clip(local_tile, 0, tile_total - 1)), 0.0)
    received = link_gain[0] * looked
    direction = lax.axis_index("dir")
    serves_here = serving == direction
    signal_part = jnp.where(serves_here, received, 0.0)
    interference_part = jnp.where(serves_here, 0.0, received)
    device_count = lax.axis_size(("dir", "row"))
    terms = jnp.stack([signal_part, interference_part]).reshape(2, device_count, -1)
    gathered = lax.all_to_all(
        terms.transpose(1, 0, 2), ("dir", "row"), split_axis=0, concat_axis=0, tiled=True
    )
    signal, interference = jnp.sum(gathered, axis=0)
    signal_ratio = jnp.log10(signal / (interference + noise_floor))
    return (fluctuation[None], signal_ratio)


def solution(mesh):
    return jax.shard_map(
        body,
        mesh=mesh,
        in_specs=(
            P(None, ("dir", "row"), None),
            P("dir", None),
            P("dir"),
            P("dir", None),
            P("dir", None),
            P(),
        ),
        out_specs=(P("dir", "row", None), P(("dir", "row"))),
        check_vma=False,
    )
```

```python
import math

import jax
import jax.numpy as jnp
import ml_dtypes
import numpy as np
from jax import lax
from jax.experimental import pallas as pl
from jax.experimental.pallas import tpu as pltpu
from jax.sharding import PartitionSpec as P

N = 8192
FIRST = 64
SECOND = 128
ROWS_DEV = 32
XTILES = 128
YTILES = 8
TILE_X = 64
GROUP = 8
CHUNKS = 4


full_turn = 2.0 * math.pi
noise_floor = 0.05
tiny_value = 1e-06
strength = 1.6
row_patterns = (
    "zrab,zwak->wrkb",
    "zrkb,zwbc->wrkc",
    "zrkc,wzbc->wrkb",
    "zrkb,wzak->wrab",
    "zrkb,zak->rab",
)
column_patterns = (
    "zaby,zwak->wkby",
    "zkby,zwbc->wkcy",
    "zkcy,wzbc->wkby",
    "zkby,wzak->waby",
    "zkby,zak->aby",
)


def complex_block(real_part, imag_part):
    return jnp.stack(
        [jnp.stack([real_part, imag_part]), jnp.stack([-imag_part, real_part])]
    ).astype(jnp.bfloat16)


def transform_tables(first, second):
    total = first * second
    outer_ids = jnp.arange(first, dtype=jnp.int32)
    inner_ids = jnp.arange(second, dtype=jnp.int32)
    outer_angle = (outer_ids[:, None] * outer_ids[None, :] % first).astype(jnp.float32) * (
        full_turn / first
    )
    inner_angle = (inner_ids[:, None] * inner_ids[None, :] % second).astype(jnp.float32) * (
        full_turn / second
    )
    twist_angle = (outer_ids[:, None] * inner_ids[None, :] % total).astype(jnp.float32) * (
        full_turn / total
    )
    return (
        complex_block(jnp.cos(outer_angle), -jnp.sin(outer_angle)),
        complex_block(jnp.cos(inner_angle), -jnp.sin(inner_angle)),
        jnp.cos(twist_angle),
        -jnp.sin(twist_angle),
    )


def signed_wave(positions, first, second):
    total = first * second
    wave_number = positions // second + first * (positions % second)
    return jnp.where(wave_number >= total // 2, wave_number - total, wave_number).astype(
        jnp.float32
    )


def spectral_filter(row_ids, column_ids):
    wave_rows = signed_wave(row_ids, FIRST, SECOND)
    wave_columns = signed_wave(column_ids, FIRST, SECOND)
    squared_radius = 16.0 + wave_rows[:, None] ** 2 + wave_columns[None, :] ** 2
    return strength * float(N) * float(N) * squared_radius ** (-0.75)


def fresnel_factor(geometry_row, first, second):
    total = first * second
    fresnel_area = 144.0 * jnp.exp2(geometry_row[0].astype(jnp.float32))
    positions = jnp.arange(total, dtype=jnp.int32).reshape(first, second)
    scaled = signed_wave(positions, first, second) * (full_turn / total)
    turning = 0.5 * scaled * scaled * fresnel_area
    return (jnp.cos(turning), -jnp.sin(turning))


def complex_times(values, real_part, imag_part):
    return jnp.stack(
        [
            values[0] * real_part - values[1] * imag_part,
            values[0] * imag_part + values[1] * real_part,
        ]
    )


def contract(pattern, operand, matrix):
    return jnp.einsum(pattern, operand, matrix, preferred_element_type=jnp.float32)


def table_length(tables):
    return tables[0].shape[2] * tables[1].shape[2]


def forward_axis(values, tables, factor, patterns, trailing):
    outer_table, inner_table, twist_real, twist_imag = tables
    factor_real, factor_imag = factor
    if trailing:
        twist_real, twist_imag = (twist_real[..., None], twist_imag[..., None])
        factor_real, factor_imag = (factor_real[..., None], factor_imag[..., None])
    section_one = complex_times(
        contract(patterns[0], values, outer_table), twist_real, twist_imag
    ).astype(jnp.bfloat16)
    section_two = contract(patterns[1], section_one, inner_table)
    return complex_times(section_two, factor_real, factor_imag).astype(jnp.bfloat16)


def inverse_first(values, tables, patterns, trailing):
    outer_table, inner_table, twist_real, twist_imag = tables
    if trailing:
        twist_real, twist_imag = (twist_real[..., None], twist_imag[..., None])
    return complex_times(
        contract(patterns[2], values, inner_table), twist_real, -twist_imag
    ).astype(jnp.bfloat16)


def inverse_axis(values, tables, patterns, trailing):
    section_one = inverse_first(values, tables, patterns, trailing)
    return contract(patterns[3], section_one, tables[0]) * (1.0 / table_length(tables))


def window_matrix(half_width):
    positions = jnp.arange(XTILES, dtype=jnp.int32)
    difference = (positions[:, None] - positions[None, :]) % XTILES
    distance = jnp.minimum(difference, XTILES - difference)
    return (distance <= half_width).astype(jnp.float32)


def tile_statistics(first_moment, second_moment, half_width, tile_rows):
    window_mask = window_matrix(half_width)
    cells = ((2 * half_width + 1) * (TILE_X * tile_rows)).astype(jnp.float32)
    mean_one = jnp.dot(first_moment, window_mask, precision=lax.Precision.HIGHEST) / cells
    mean_two = jnp.dot(second_moment, window_mask, precision=lax.Precision.HIGHEST) / cells
    fluctuation = mean_two / (mean_one * mean_one + tiny_value) - 1.0
    return (fluctuation, mean_one * jnp.exp(-fluctuation))


def propagate_columns(phase_patch, tables_y, slant_factor, fresnel_y):
    patch_rows = phase_patch.shape[0]
    width_here = phase_patch.shape[1]
    outer_len = tables_y[0].shape[2]
    inner_len = tables_y[1].shape[2]
    turned_phase = slant_factor * phase_patch
    screen_field = jnp.stack([jnp.cos(turned_phase), jnp.sin(turned_phase)]).astype(jnp.bfloat16)
    stacked = screen_field.reshape(2, outer_len, inner_len, width_here)
    spectral = forward_axis(stacked, tables_y, fresnel_y, column_patterns, True)
    result = inverse_axis(spectral, tables_y, column_patterns, True)
    return result.astype(jnp.bfloat16).reshape(2, patch_rows, width_here)


def half_screen_rows(white_noise, row_start, tables):
    rows_here = white_noise.shape[1]
    row_ids = row_start + jnp.arange(rows_here, dtype=jnp.int32)
    column_ids = jnp.arange(N, dtype=jnp.int32)
    spectral_gain = spectral_filter(row_ids, column_ids)
    spectrum = (white_noise.astype(jnp.float32) * spectral_gain).astype(jnp.bfloat16)
    half_screen = inverse_axis(
        spectrum.reshape(2, rows_here, FIRST, SECOND), tables, row_patterns, False
    )
    half_screen = half_screen.astype(jnp.bfloat16).reshape(2, rows_here, N)
    return half_screen


def gathered_patch(half_screen, geometry, tables, patch_len):
    turned = lax.all_to_all(half_screen, "row", split_axis=2, concat_axis=1, tiled=True)
    band_rows = turned.shape[1]
    columns = turned.shape[2]
    offset_rows = N // 4 * geometry[0, 1]
    blocks = band_rows // SECOND
    block_start = lax.axis_index("dir") * blocks
    stacked = turned.reshape(2, blocks, SECOND, columns)
    twist_real = lax.dynamic_slice_in_dim(tables[2], block_start, blocks, 0)[..., None]
    twist_imag = lax.dynamic_slice_in_dim(tables[3], block_start, blocks, 0)[..., None]
    section_one = complex_times(
        contract("zkcx,wzbc->wkbx", stacked, tables[1]), twist_real, -twist_imag
    )
    section_one = section_one.astype(jnp.bfloat16)
    outer_count = patch_len // SECOND
    outer_ids = (offset_rows // SECOND + jnp.arange(outer_count, dtype=jnp.int32)) % FIRST
    patch_outer = jnp.take(tables[0][0], outer_ids, axis=1)
    phase_patch = contract(
        "zkbx,zak->abx", lax.all_gather(section_one, "dir", axis=1, tiled=True), patch_outer
    )
    return phase_patch.reshape(patch_len, columns) * (1.0 / N)


def host_tables():
    def block(length):
        ids = np.arange(length)
        angle = (ids[:, None] * ids[None, :] % length) * (full_turn / length)
        real_part, imag_part = (np.cos(angle), np.sin(angle))
        return np.array([[real_part, -imag_part], [imag_part, real_part]])

    inner = block(SECOND).transpose(1, 3, 0, 2).reshape(2 * SECOND, 2 * SECOND)
    outer = block(FIRST).transpose(0, 2, 1, 3).reshape(2 * FIRST, 2 * FIRST)
    spread = np.kron(outer, np.eye(GROUP))
    twist = np.arange(FIRST)[:, None] * np.arange(SECOND)[None, :] * (full_turn / N)
    twist = np.repeat(twist, GROUP, axis=0)
    angle = (np.arange(SECOND)[:, None] * np.arange(SECOND)[None, :] % SECOND) * (full_turn / SECOND)
    return (
        inner.astype(ml_dtypes.bfloat16),
        np.stack([np.cos(twist), np.sin(twist)]).astype(np.float32),
        spread.astype(ml_dtypes.bfloat16),
        np.stack([np.cos(angle), np.sin(angle)]).astype(np.float32),
    )


def screen_kernel(
    spot, noise, rows_squared, columns_squared, inner, twist, spread, kept, moved, staged
):
    core, y_spot = (spot[0], spot[1])
    root = lax.rsqrt(16.0 + rows_squared[...] + columns_squared[...])
    gain = strength * root * (root * lax.rsqrt(root))
    spectrum = [noise[z].astype(jnp.float32) * gain for z in range(2)]
    sections = []
    for group in range(2):
        rows = slice(group * GROUP, (group + 1) * GROUP)
        parts = [
            jnp.concatenate(
                [spectrum[z][rows, k * SECOND : (k + 1) * SECOND] for k in range(FIRST)], axis=0
            ).astype(jnp.bfloat16)
            for z in range(2)
        ]
        first = jnp.dot(
            jnp.concatenate(parts, axis=1), inner[...], preferred_element_type=jnp.float32
        )
        real_part, imag_part = (first[:, :SECOND], first[:, SECOND:])
        turned = jnp.concatenate(
            [
                real_part * twist[0] - imag_part * twist[1],
                real_part * twist[1] + imag_part * twist[0],
            ],
            axis=0,
        )
        sections.append(turned.astype(jnp.bfloat16))
    staged[...] = jnp.dot(
        spread[...], jnp.concatenate(sections, axis=1), preferred_element_type=jnp.float32
    )
    for core_side, target in enumerate((kept, moved)):
        for y_side in range(2):
            for chunk in range(CHUNKS):
                for z_spot in range(4):
                    place = z_spot * 4 + (y_spot ^ y_side) * 2 + (core ^ core_side)
                    for w in range(2):
                        start = (w * FIRST + place * CHUNKS + chunk) * GROUP
                        taken = staged[pl.ds(pl.multiple_of(start, GROUP), GROUP), :]
                        both = jnp.concatenate([taken[:, :SECOND], taken[:, SECOND:]], axis=0)
                        target[y_side, chunk, w, :, z_spot * SECOND : (z_spot + 1) * SECOND] = (
                            both.astype(jnp.bfloat16)
                        )


def half_screens(white_noise, row_start, row, host):
    rows_here = white_noise.shape[1]
    inner, twist, spread, _ = host
    row_waves = signed_wave(row_start + jnp.arange(rows_here, dtype=jnp.int32), FIRST, SECOND)
    column_waves = signed_wave(jnp.arange(N, dtype=jnp.int32), FIRST, SECOND)
    spot = jnp.stack([row % 2, row // 2 % 2])
    step = 2 * GROUP
    out_shape = (2, CHUNKS, 2, rows_here, 4 * SECOND)
    out_spec = pl.BlockSpec((2, CHUNKS, 2, step, 4 * SECOND), lambda i: (0, 0, 0, i, 0))

    def whole(array):
        return pl.BlockSpec(array.shape, lambda i: (0,) * array.ndim)

    return pl.pallas_call(
        screen_kernel,
        grid=(rows_here // step,),
        in_specs=[
            pl.BlockSpec(memory_space=pltpu.SMEM),
            pl.BlockSpec((2, step, N), lambda i: (0, i, 0)),
            pl.BlockSpec((step, 1), lambda i: (i, 0)),
            pl.BlockSpec((1, N), lambda i: (0, 0)),
            whole(inner),
            whole(twist),
            whole(spread),
        ],
        out_specs=[out_spec, out_spec],
        out_shape=[jax.ShapeDtypeStruct(out_shape, jnp.bfloat16)] * 2,
        scratch_shapes=[pltpu.VMEM((2 * FIRST * GROUP, 2 * SECOND), jnp.float32)],
        compiler_params=pltpu.CompilerParams(vmem_limit_bytes=48 * 1024 * 1024),
        cost_estimate=pl.CostEstimate(
            flops=20_000_000_000, bytes_accessed=20_000_000, transcendentals=4_000_000
        ),
    )(
        spot,
        white_noise,
        (row_waves * row_waves)[:, None],
        (column_waves * column_waves)[None, :],
        inner,
        twist,
        spread,
    )


def matrix_kernel(slow, fast, matrix):
    for source in range(2):
        for near in range(2):
            block = source * 2 + near
            slow_real = slow[0, :, block : block + 1]
            slow_imag = slow[1, :, block : block + 1]
            real_part = slow_real * fast[0] - slow_imag * fast[1]
            imag_part = slow_real * fast[1] + slow_imag * fast[0]
            for z, part in enumerate((real_part, -imag_part)):
                start = ((source * 2 + z) * 2 + near) * SECOND
                matrix[:, start : start + SECOND] = part.astype(jnp.bfloat16)


def patch_matrix(slant_bins, block_ids, outer_count, fast):
    inner_ids = jnp.arange(SECOND, dtype=jnp.int32)
    outer_ids = slant_bins[:, None] * (FIRST // 4) + jnp.arange(outer_count, dtype=jnp.int32)
    position = (outer_ids[:, :, None] * SECOND + inner_ids).reshape(-1)
    slow = (position[:, None] * block_ids[None, :] % N).astype(jnp.float32) * (full_turn / N)
    slow = jnp.stack([jnp.cos(slow), jnp.sin(slow)])
    length = position.shape[0]
    return pl.pallas_call(
        matrix_kernel,
        grid=(length // SECOND,),
        in_specs=[
            pl.BlockSpec((2, SECOND, 4), lambda i: (0, i, 0)),
            pl.BlockSpec(fast.shape, lambda i: (0, 0, 0)),
        ],
        out_specs=pl.BlockSpec((SECOND, 8 * SECOND), lambda i: (i, 0)),
        out_shape=jax.ShapeDtypeStruct((length, 8 * SECOND), jnp.bfloat16),
        cost_estimate=pl.CostEstimate(
            flops=8_000_000, bytes_accessed=4_000_000, transcendentals=0
        ),
    )(slow, fast)


def product_kernel(matrix, kept, received, result):
    depth = kept.shape[0] * kept.shape[1]
    columns = kept.shape[2]
    total = jnp.dot(
        matrix[:, :depth],
        kept[...].reshape(depth, columns),
        preferred_element_type=jnp.float32,
    )
    total += jnp.dot(
        matrix[:, depth:],
        received[...].reshape(depth, columns),
        preferred_element_type=jnp.float32,
    )
    result[...] = total.astype(result.dtype).reshape(result.shape)


def patch_products(matrix, kept, received):
    patch_len = matrix.shape[0] // 2
    sides, chunks, parts, rows, columns = kept.shape
    values_spec = pl.BlockSpec(
        (None, None, parts, rows, columns), lambda i, j: (j, i, 0, 0, 0)
    )
    return pl.pallas_call(
        product_kernel,
        grid=(chunks, sides),
        in_specs=[
            pl.BlockSpec(matrix.shape, lambda i, j: (0, 0)),
            values_spec,
            values_spec,
        ],
        out_specs=pl.BlockSpec(
            (None, 2, None, patch_len, columns), lambda i, j: (i, 0, j, 0, 0)
        ),
        out_shape=jax.ShapeDtypeStruct((chunks, 2, sides, patch_len, columns), jnp.bfloat16),
        compiler_params=pltpu.CompilerParams(vmem_limit_bytes=32 * 1024 * 1024),
        cost_estimate=pl.CostEstimate(
            flops=9_000_000_000, bytes_accessed=20_000_000, transcendentals=0
        ),
    )(matrix, kept, received)


def reduce_kernel(
    products, result, a_recv, b_send, b_recv, z_send, z_recv, a_sems, b_sems, z_sems
):
    here_x, row = (lax.axis_index("dir"), lax.axis_index("row"))
    z_spot, y_spot = (row // 4, row // 2 % 2)
    x_mate = (1 - here_x, row)
    y_mate = (here_x, row + 2 - 4 * y_spot)
    z_spots = [(z_spot + shift) % 4 for shift in range(1, 4)]
    z_mates = [(here_x, row + 4 * (spot - z_spot)) for spot in z_spots]
    mates = [x_mate, y_mate] + z_mates
    barrier = pltpu.get_barrier_semaphore()
    for mate in mates:
        pl.semaphore_signal(barrier, inc=1, device_id=mate, device_id_type=pl.DeviceIdType.MESH)
    pl.semaphore_wait(barrier, len(mates))

    height = a_recv.shape[2]
    units = [
        (2 * pair + way, half) for pair in range(2) for half in range(2) for way in range(2)
    ]

    def copy(source, target, sems, spot, mate):
        return pltpu.make_async_remote_copy(
            src_ref=source,
            dst_ref=target,
            send_sem=sems.at[(0, *spot)],
            recv_sem=sems.at[(1, *spot)],
            device_id=mate,
            device_id_type=pl.DeviceIdType.MESH,
        )

    def rows_of(unit):
        return pl.ds(units[unit][1] * height, height)

    a_copies, b_copies, z_copies = ([], [], [])
    for unit, (chunk, _) in enumerate(units):
        rows = rows_of(unit)
        if chunk % 2 == 0:
            source = products.at[chunk, 1, :, rows, :]
            first_mate, second_mate = (x_mate, y_mate)
        else:
            source = products.at[chunk, :, 1, rows, :]
            first_mate, second_mate = (y_mate, x_mate)
        a_copies.append(copy(source, a_recv.at[unit], a_sems, (unit,), first_mate))
        b_copies.append(copy(b_send.at[unit], b_recv.at[unit], b_sems, (unit,), second_mate))
        z_copies.append(
            [
                copy(
                    z_send.at[unit, z_spots[shift]],
                    z_recv.at[unit, shift],
                    z_sems,
                    (unit, shift),
                    z_mates[shift],
                )
                for shift in range(3)
            ]
        )

    def finish(unit):
        chunk, _ = units[unit]
        b_copies[unit].wait_recv()
        total = (
            products[chunk, 0, 0, rows_of(unit), :].astype(jnp.float32)
            + a_recv[unit, 0].astype(jnp.float32)
            + b_recv[unit].astype(jnp.float32)
        ).astype(jnp.bfloat16)
        for spot in range(4):
            z_send[unit, spot] = total[:, spot * SECOND : (spot + 1) * SECOND]
        for sent in z_copies[unit]:
            sent.start()

    count = len(units)
    ahead = 4
    for unit in range(ahead):
        a_copies[unit].start()
    for unit, (chunk, _) in enumerate(units):
        a_copies[unit].wait_recv()
        side = (0, 1) if chunk % 2 == 0 else (1, 0)
        b_send[unit] = (
            products[chunk, side[0], side[1], rows_of(unit), :].astype(jnp.float32)
            + a_recv[unit, 1].astype(jnp.float32)
        ).astype(jnp.bfloat16)
        b_copies[unit].start()
        if unit + ahead < count:
            a_copies[unit + ahead].start()
        if unit >= 2:
            finish(unit - 2)
    finish(count - 2)
    finish(count - 1)
    for unit, (chunk, _) in enumerate(units):
        total = z_send[unit, z_spot].astype(jnp.float32)
        for shift in range(3):
            z_copies[unit][shift].wait_recv()
            total += z_recv[unit, shift].astype(jnp.float32)
        result[rows_of(unit), chunk * SECOND : (chunk + 1) * SECOND] = total
    for unit in range(count):
        a_copies[unit].wait_send()
        b_copies[unit].wait_send()
        for sent in z_copies[unit]:
            sent.wait_send()


def reduce_products(products):
    chunks, _, _, patch_len, columns = products.shape
    count, height = (2 * chunks, patch_len // 2)
    held = jnp.bfloat16
    return pl.pallas_call(
        reduce_kernel,
        in_specs=[pl.BlockSpec(memory_space=pltpu.VMEM)],
        out_specs=pl.BlockSpec(memory_space=pltpu.VMEM),
        out_shape=jax.ShapeDtypeStruct((patch_len, chunks * SECOND), jnp.float32),
        scratch_shapes=[
            pltpu.VMEM((count, 2, height, columns), held),
            pltpu.VMEM((count, height, columns), held),
            pltpu.VMEM((count, height, columns), held),
            pltpu.VMEM((count, 4, height, SECOND), held),
            pltpu.VMEM((count, 3, height, SECOND), held),
            pltpu.SemaphoreType.DMA((2, count)),
            pltpu.SemaphoreType.DMA((2, count)),
            pltpu.SemaphoreType.DMA((2, count, 3)),
        ],
        compiler_params=pltpu.CompilerParams(
            collective_id=0, has_side_effects=True, vmem_limit_bytes=40 * 1024 * 1024
        ),
    )(products)


def reduced_patch(white_noise, row_start, geometry):
    row_count = lax.axis_size("row")
    patch_len = row_count * ROWS_DEV
    row = lax.axis_index("row")
    over_core = [(r, r ^ 1) for r in range(row_count)]
    host = host_tables()
    kept, moved = half_screens(white_noise, row_start, row, host)
    received = lax.ppermute(moved, "row", over_core)
    slant_bin, kept = lax.optimization_barrier((geometry[0, 1], kept))
    other_bin = lax.ppermute(slant_bin, "dir", [(0, 1), (1, 0)])
    first_block = 2 * (lax.axis_index("dir") * row_count + row)
    other_block = 2 * (lax.axis_index("dir") * row_count + (row ^ 1))
    block_ids = jnp.stack([first_block, first_block + 1, other_block, other_block + 1])
    slant_bins = jnp.stack([slant_bin, other_bin])
    matrix = patch_matrix(slant_bins, block_ids, patch_len // SECOND, host[3])
    return reduce_products(patch_products(matrix, kept, received))


def body(white_noise, geometry, window, tile_map, link_gain, serving):
    row_count = lax.axis_size("row")
    tables = transform_tables(FIRST, SECOND)
    tables_y = transform_tables(row_count, ROWS_DEV)
    patch_len = row_count * ROWS_DEV
    rows_here = white_noise.shape[1]
    row_start = lax.axis_index(("dir", "row")) * rows_here
    slant_factor = 1.0 + 0.25 * geometry[0, 1].astype(jnp.float32)
    fresnel_x = fresnel_factor(geometry[0], FIRST, SECOND)
    fresnel_y = fresnel_factor(geometry[0], row_count, ROWS_DEV)
    if lax.axis_size("dir") == 2 and row_count == 16 and rows_here == 2 * SECOND:
        phase_patch = reduced_patch(white_noise, row_start, geometry)
    else:
        half_screen = half_screen_rows(white_noise, row_start, tables)
        phase_patch = gathered_patch(half_screen, geometry, tables, patch_len)
    columns = phase_patch.shape[1]
    screen_field = propagate_columns(phase_patch, tables_y, slant_factor, fresnel_y)
    stacked_field = screen_field.reshape(2, row_count, ROWS_DEV, columns)
    portion = lax.all_to_all(stacked_field, "row", split_axis=1, concat_axis=3, tiled=True)
    item_count = portion.shape[2]
    stacked = portion.reshape(2, item_count, FIRST, SECOND)
    spectral = forward_axis(stacked, tables, fresnel_x, row_patterns, False)
    wave_field = inverse_axis(spectral, tables, row_patterns, False)
    intensity = wave_field[0] * wave_field[0] + wave_field[1] * wave_field[1]
    intensity = intensity.reshape(item_count, XTILES, TILE_X)
    tile_one = jnp.sum(intensity, axis=2)
    tile_two = jnp.sum(intensity * intensity, axis=2)
    tile_rows = ROWS_DEV // YTILES
    first_moment = jnp.sum(tile_one.reshape(YTILES, tile_rows, XTILES), axis=1)
    second_moment = jnp.sum(tile_two.reshape(YTILES, tile_rows, XTILES), axis=1)
    fluctuation, faded_power = tile_statistics(first_moment, second_moment, window[0], tile_rows)
    faded_flat = faded_power.reshape(-1)
    tile_total = faded_flat.shape[0]
    local_tile = tile_map[0] - lax.axis_index("row") * tile_total
    inside = (local_tile >= 0) & (local_tile < tile_total)
    looked = jnp.where(inside, jnp.take(faded_flat, jnp.clip(local_tile, 0, tile_total - 1)), 0.0)
    received = link_gain[0] * looked
    direction = lax.axis_index("dir")
    serves_here = serving == direction
    signal_part = jnp.where(serves_here, received, 0.0)
    interference_part = jnp.where(serves_here, 0.0, received)
    device_count = lax.axis_size(("dir", "row"))
    terms = jnp.stack([signal_part, interference_part]).reshape(2, device_count, -1)
    gathered = lax.all_to_all(
        terms.transpose(1, 0, 2), ("dir", "row"), split_axis=0, concat_axis=0, tiled=True
    )
    signal, interference = jnp.sum(gathered, axis=0)
    signal_ratio = jnp.log10(signal / (interference + noise_floor))
    return (fluctuation[None], signal_ratio)


def solution(mesh):
    return jax.shard_map(
        body,
        mesh=mesh,
        in_specs=(
            P(None, ("dir", "row"), None),
            P("dir", None),
            P("dir"),
            P("dir", None),
            P("dir", None),
            P(),
        ),
        out_specs=(P("dir", "row", None), P(("dir", "row"))),
        check_vma=False,
    )
```

```python
import math

import jax
import jax.numpy as jnp
import ml_dtypes
import numpy as np
from jax import lax
from jax.experimental import pallas as pl
from jax.experimental.pallas import tpu as pltpu
from jax.sharding import PartitionSpec as P

N = 8192
FIRST = 64
SECOND = 128
ROWS_DEV = 32
XTILES = 128
YTILES = 8
TILE_X = 64
GROUP = 8
CHUNKS = 4


full_turn = 2.0 * math.pi
noise_floor = 0.05
tiny_value = 1e-06
strength = 1.6
row_patterns = (
    "zrab,zwak->wrkb",
    "zrkb,zwbc->wrkc",
    "zrkc,wzbc->wrkb",
    "zrkb,wzak->wrab",
    "zrkb,zak->rab",
)
column_patterns = (
    "zaby,zwak->wkby",
    "zkby,zwbc->wkcy",
    "zkcy,wzbc->wkby",
    "zkby,wzak->waby",
    "zkby,zak->aby",
)


def complex_block(real_part, imag_part):
    return jnp.stack(
        [jnp.stack([real_part, imag_part]), jnp.stack([-imag_part, real_part])]
    ).astype(jnp.bfloat16)


def transform_tables(first, second):
    total = first * second
    outer_ids = jnp.arange(first, dtype=jnp.int32)
    inner_ids = jnp.arange(second, dtype=jnp.int32)
    outer_angle = (outer_ids[:, None] * outer_ids[None, :] % first).astype(jnp.float32) * (
        full_turn / first
    )
    inner_angle = (inner_ids[:, None] * inner_ids[None, :] % second).astype(jnp.float32) * (
        full_turn / second
    )
    twist_angle = (outer_ids[:, None] * inner_ids[None, :] % total).astype(jnp.float32) * (
        full_turn / total
    )
    return (
        complex_block(jnp.cos(outer_angle), -jnp.sin(outer_angle)),
        complex_block(jnp.cos(inner_angle), -jnp.sin(inner_angle)),
        jnp.cos(twist_angle),
        -jnp.sin(twist_angle),
    )


def signed_wave(positions, first, second):
    total = first * second
    wave_number = positions // second + first * (positions % second)
    return jnp.where(wave_number >= total // 2, wave_number - total, wave_number).astype(
        jnp.float32
    )


def spectral_filter(row_ids, column_ids):
    wave_rows = signed_wave(row_ids, FIRST, SECOND)
    wave_columns = signed_wave(column_ids, FIRST, SECOND)
    squared_radius = 16.0 + wave_rows[:, None] ** 2 + wave_columns[None, :] ** 2
    return strength * float(N) * float(N) * squared_radius ** (-0.75)


def fresnel_factor(geometry_row, first, second):
    total = first * second
    fresnel_area = 144.0 * jnp.exp2(geometry_row[0].astype(jnp.float32))
    positions = jnp.arange(total, dtype=jnp.int32).reshape(first, second)
    scaled = signed_wave(positions, first, second) * (full_turn / total)
    turning = 0.5 * scaled * scaled * fresnel_area
    return (jnp.cos(turning), -jnp.sin(turning))


def complex_times(values, real_part, imag_part):
    return jnp.stack(
        [
            values[0] * real_part - values[1] * imag_part,
            values[0] * imag_part + values[1] * real_part,
        ]
    )


def contract(pattern, operand, matrix):
    return jnp.einsum(pattern, operand, matrix, preferred_element_type=jnp.float32)


def table_length(tables):
    return tables[0].shape[2] * tables[1].shape[2]


def forward_axis(values, tables, factor, patterns, trailing):
    outer_table, inner_table, twist_real, twist_imag = tables
    factor_real, factor_imag = factor
    if trailing:
        twist_real, twist_imag = (twist_real[..., None], twist_imag[..., None])
        factor_real, factor_imag = (factor_real[..., None], factor_imag[..., None])
    section_one = complex_times(
        contract(patterns[0], values, outer_table), twist_real, twist_imag
    ).astype(jnp.bfloat16)
    section_two = contract(patterns[1], section_one, inner_table)
    return complex_times(section_two, factor_real, factor_imag).astype(jnp.bfloat16)


def inverse_first(values, tables, patterns, trailing):
    outer_table, inner_table, twist_real, twist_imag = tables
    if trailing:
        twist_real, twist_imag = (twist_real[..., None], twist_imag[..., None])
    return complex_times(
        contract(patterns[2], values, inner_table), twist_real, -twist_imag
    ).astype(jnp.bfloat16)


def inverse_axis(values, tables, patterns, trailing):
    section_one = inverse_first(values, tables, patterns, trailing)
    return contract(patterns[3], section_one, tables[0]) * (1.0 / table_length(tables))


def window_matrix(half_width):
    positions = jnp.arange(XTILES, dtype=jnp.int32)
    difference = (positions[:, None] - positions[None, :]) % XTILES
    distance = jnp.minimum(difference, XTILES - difference)
    return (distance <= half_width).astype(jnp.float32)


def tile_statistics(first_moment, second_moment, half_width, tile_rows):
    window_mask = window_matrix(half_width)
    cells = ((2 * half_width + 1) * (TILE_X * tile_rows)).astype(jnp.float32)
    mean_one = jnp.dot(first_moment, window_mask, precision=lax.Precision.HIGHEST) / cells
    mean_two = jnp.dot(second_moment, window_mask, precision=lax.Precision.HIGHEST) / cells
    fluctuation = mean_two / (mean_one * mean_one + tiny_value) - 1.0
    return (fluctuation, mean_one * jnp.exp(-fluctuation))


def propagate_columns(phase_patch, tables_y, slant_factor, fresnel_y):
    patch_rows = phase_patch.shape[0]
    width_here = phase_patch.shape[1]
    outer_len = tables_y[0].shape[2]
    inner_len = tables_y[1].shape[2]
    turned_phase = slant_factor * phase_patch
    screen_field = jnp.stack([jnp.cos(turned_phase), jnp.sin(turned_phase)]).astype(jnp.bfloat16)
    stacked = screen_field.reshape(2, outer_len, inner_len, width_here)
    spectral = forward_axis(stacked, tables_y, fresnel_y, column_patterns, True)
    result = inverse_axis(spectral, tables_y, column_patterns, True)
    return result.astype(jnp.bfloat16).reshape(2, patch_rows, width_here)


def half_screen_rows(white_noise, row_start, tables):
    rows_here = white_noise.shape[1]
    row_ids = row_start + jnp.arange(rows_here, dtype=jnp.int32)
    column_ids = jnp.arange(N, dtype=jnp.int32)
    spectral_gain = spectral_filter(row_ids, column_ids)
    spectrum = (white_noise.astype(jnp.float32) * spectral_gain).astype(jnp.bfloat16)
    half_screen = inverse_axis(
        spectrum.reshape(2, rows_here, FIRST, SECOND), tables, row_patterns, False
    )
    half_screen = half_screen.astype(jnp.bfloat16).reshape(2, rows_here, N)
    return half_screen


def gathered_patch(half_screen, geometry, tables, patch_len):
    turned = lax.all_to_all(half_screen, "row", split_axis=2, concat_axis=1, tiled=True)
    band_rows = turned.shape[1]
    columns = turned.shape[2]
    offset_rows = N // 4 * geometry[0, 1]
    blocks = band_rows // SECOND
    block_start = lax.axis_index("dir") * blocks
    stacked = turned.reshape(2, blocks, SECOND, columns)
    twist_real = lax.dynamic_slice_in_dim(tables[2], block_start, blocks, 0)[..., None]
    twist_imag = lax.dynamic_slice_in_dim(tables[3], block_start, blocks, 0)[..., None]
    section_one = complex_times(
        contract("zkcx,wzbc->wkbx", stacked, tables[1]), twist_real, -twist_imag
    )
    section_one = section_one.astype(jnp.bfloat16)
    outer_count = patch_len // SECOND
    outer_ids = (offset_rows // SECOND + jnp.arange(outer_count, dtype=jnp.int32)) % FIRST
    patch_outer = jnp.take(tables[0][0], outer_ids, axis=1)
    phase_patch = contract(
        "zkbx,zak->abx", lax.all_gather(section_one, "dir", axis=1, tiled=True), patch_outer
    )
    return phase_patch.reshape(patch_len, columns) * (1.0 / N)


def host_tables():
    def block(length):
        ids = np.arange(length)
        angle = (ids[:, None] * ids[None, :] % length) * (full_turn / length)
        real_part, imag_part = (np.cos(angle), np.sin(angle))
        return np.array([[real_part, -imag_part], [imag_part, real_part]])

    inner = block(SECOND).transpose(1, 3, 0, 2).reshape(2 * SECOND, 2 * SECOND)
    outer = block(FIRST).transpose(0, 2, 1, 3).reshape(2 * FIRST, 2 * FIRST)
    spread = np.kron(outer, np.eye(GROUP))
    twist = np.arange(FIRST)[:, None] * np.arange(SECOND)[None, :] * (full_turn / N)
    twist = np.repeat(twist, GROUP, axis=0)
    angle = (np.arange(SECOND)[:, None] * np.arange(SECOND)[None, :] % SECOND) * (full_turn / SECOND)
    return (
        inner.astype(ml_dtypes.bfloat16),
        np.stack([np.cos(twist), np.sin(twist)]).astype(np.float32),
        spread.astype(ml_dtypes.bfloat16),
        np.stack([np.cos(angle), np.sin(angle)]).astype(np.float32),
    )


def screen_kernel(
    spot, noise, rows_squared, columns_squared, inner, twist, spread, kept, moved, staged
):
    core, y_spot = (spot[0], spot[1])
    root = lax.rsqrt(16.0 + rows_squared[...] + columns_squared[...])
    gain = strength * root * (root * lax.rsqrt(root))
    spectrum = [noise[z].astype(jnp.float32) * gain for z in range(2)]
    sections = []
    for group in range(2):
        rows = slice(group * GROUP, (group + 1) * GROUP)
        parts = [
            jnp.concatenate(
                [spectrum[z][rows, k * SECOND : (k + 1) * SECOND] for k in range(FIRST)], axis=0
            ).astype(jnp.bfloat16)
            for z in range(2)
        ]
        first = jnp.dot(
            jnp.concatenate(parts, axis=1), inner[...], preferred_element_type=jnp.float32
        )
        real_part, imag_part = (first[:, :SECOND], first[:, SECOND:])
        turned = jnp.concatenate(
            [
                real_part * twist[0] - imag_part * twist[1],
                real_part * twist[1] + imag_part * twist[0],
            ],
            axis=0,
        )
        sections.append(turned.astype(jnp.bfloat16))
    staged[...] = jnp.dot(
        spread[...], jnp.concatenate(sections, axis=1), preferred_element_type=jnp.float32
    )
    for core_side, target in enumerate((kept, moved)):
        for y_side in range(2):
            for chunk in range(CHUNKS):
                for z_spot in range(4):
                    place = z_spot * 4 + (y_spot ^ y_side) * 2 + (core ^ core_side)
                    for w in range(2):
                        start = (w * FIRST + place * CHUNKS + chunk) * GROUP
                        taken = staged[pl.ds(pl.multiple_of(start, GROUP), GROUP), :]
                        both = jnp.concatenate([taken[:, :SECOND], taken[:, SECOND:]], axis=0)
                        target[y_side, chunk, w, :, z_spot * SECOND : (z_spot + 1) * SECOND] = (
                            both.astype(jnp.bfloat16)
                        )


def half_screens(white_noise, row_start, row, host):
    rows_here = white_noise.shape[1]
    inner, twist, spread, _ = host
    row_waves = signed_wave(row_start + jnp.arange(rows_here, dtype=jnp.int32), FIRST, SECOND)
    column_waves = signed_wave(jnp.arange(N, dtype=jnp.int32), FIRST, SECOND)
    spot = jnp.stack([row % 2, row // 2 % 2])
    step = 2 * GROUP
    out_shape = (2, CHUNKS, 2, rows_here, 4 * SECOND)
    out_spec = pl.BlockSpec((2, CHUNKS, 2, step, 4 * SECOND), lambda i: (0, 0, 0, i, 0))

    def whole(array):
        return pl.BlockSpec(array.shape, lambda i: (0,) * array.ndim)

    return pl.pallas_call(
        screen_kernel,
        grid=(rows_here // step,),
        in_specs=[
            pl.BlockSpec(memory_space=pltpu.SMEM),
            pl.BlockSpec((2, step, N), lambda i: (0, i, 0)),
            pl.BlockSpec((step, 1), lambda i: (i, 0)),
            pl.BlockSpec((1, N), lambda i: (0, 0)),
            whole(inner),
            whole(twist),
            whole(spread),
        ],
        out_specs=[out_spec, out_spec],
        out_shape=[jax.ShapeDtypeStruct(out_shape, jnp.bfloat16)] * 2,
        scratch_shapes=[pltpu.VMEM((2 * FIRST * GROUP, 2 * SECOND), jnp.float32)],
        compiler_params=pltpu.CompilerParams(vmem_limit_bytes=48 * 1024 * 1024),
        cost_estimate=pl.CostEstimate(
            flops=20_000_000_000, bytes_accessed=20_000_000, transcendentals=4_000_000
        ),
    )(
        spot,
        white_noise,
        (row_waves * row_waves)[:, None],
        (column_waves * column_waves)[None, :],
        inner,
        twist,
        spread,
    )


def matrix_kernel(slow, fast, matrix):
    for source in range(2):
        for near in range(2):
            block = source * 2 + near
            slow_real = slow[0, :, block : block + 1]
            slow_imag = slow[1, :, block : block + 1]
            real_part = slow_real * fast[0] - slow_imag * fast[1]
            imag_part = slow_real * fast[1] + slow_imag * fast[0]
            for z, part in enumerate((real_part, -imag_part)):
                start = ((source * 2 + z) * 2 + near) * SECOND
                matrix[:, start : start + SECOND] = part.astype(jnp.bfloat16)


def patch_matrix(slant_bins, block_ids, outer_count, fast):
    inner_ids = jnp.arange(SECOND, dtype=jnp.int32)
    outer_ids = slant_bins[:, None] * (FIRST // 4) + jnp.arange(outer_count, dtype=jnp.int32)
    position = (outer_ids[:, :, None] * SECOND + inner_ids).reshape(-1)
    slow = (position[:, None] * block_ids[None, :] % N).astype(jnp.float32) * (full_turn / N)
    slow = jnp.stack([jnp.cos(slow), jnp.sin(slow)])
    length = position.shape[0]
    return pl.pallas_call(
        matrix_kernel,
        grid=(length // SECOND,),
        in_specs=[
            pl.BlockSpec((2, SECOND, 4), lambda i: (0, i, 0)),
            pl.BlockSpec(fast.shape, lambda i: (0, 0, 0)),
        ],
        out_specs=pl.BlockSpec((SECOND, 8 * SECOND), lambda i: (i, 0)),
        out_shape=jax.ShapeDtypeStruct((length, 8 * SECOND), jnp.bfloat16),
        cost_estimate=pl.CostEstimate(
            flops=8_000_000, bytes_accessed=4_000_000, transcendentals=0
        ),
    )(slow, fast)


def product_kernel(matrix, kept, received, result):
    depth = kept.shape[0] * kept.shape[1]
    columns = kept.shape[2]
    total = jnp.dot(
        matrix[:, :depth],
        kept[...].reshape(depth, columns),
        preferred_element_type=jnp.float32,
    )
    total += jnp.dot(
        matrix[:, depth:],
        received[...].reshape(depth, columns),
        preferred_element_type=jnp.float32,
    )
    result[...] = total.astype(result.dtype).reshape(result.shape)


def patch_products(matrix, kept, received):
    patch_len = matrix.shape[0] // 2
    sides, chunks, parts, rows, columns = kept.shape
    values_spec = pl.BlockSpec(
        (None, None, parts, rows, columns), lambda i, j: (j, i, 0, 0, 0)
    )
    return pl.pallas_call(
        product_kernel,
        grid=(chunks, sides),
        in_specs=[
            pl.BlockSpec(matrix.shape, lambda i, j: (0, 0)),
            values_spec,
            values_spec,
        ],
        out_specs=pl.BlockSpec(
            (None, 2, None, patch_len, columns), lambda i, j: (i, 0, j, 0, 0)
        ),
        out_shape=jax.ShapeDtypeStruct((chunks, 2, sides, patch_len, columns), jnp.bfloat16),
        compiler_params=pltpu.CompilerParams(vmem_limit_bytes=32 * 1024 * 1024),
        cost_estimate=pl.CostEstimate(
            flops=9_000_000_000, bytes_accessed=20_000_000, transcendentals=0
        ),
    )(matrix, kept, received)


def reduce_kernel(
    products, result, a_recv, b_send, b_recv, z_send, z_recv, a_sems, b_sems, z_sems
):
    here_x, row = (lax.axis_index("dir"), lax.axis_index("row"))
    z_spot, y_spot = (row // 4, row // 2 % 2)
    x_mate = (1 - here_x, row)
    y_mate = (here_x, row + 2 - 4 * y_spot)
    z_spots = [(z_spot + shift) % 4 for shift in range(1, 4)]
    z_mates = [(here_x, row + 4 * (spot - z_spot)) for spot in z_spots]
    mates = [x_mate, y_mate] + z_mates
    barrier = pltpu.get_barrier_semaphore()
    for mate in mates:
        pl.semaphore_signal(barrier, inc=1, device_id=mate, device_id_type=pl.DeviceIdType.MESH)
    pl.semaphore_wait(barrier, len(mates))

    height = a_recv.shape[2]
    units = [
        (2 * pair + way, half) for pair in range(2) for half in range(2) for way in range(2)
    ]

    def copy(source, target, sems, spot, mate):
        return pltpu.make_async_remote_copy(
            src_ref=source,
            dst_ref=target,
            send_sem=sems.at[(0, *spot)],
            recv_sem=sems.at[(1, *spot)],
            device_id=mate,
            device_id_type=pl.DeviceIdType.MESH,
        )

    def rows_of(unit):
        return pl.ds(units[unit][1] * height, height)

    a_copies, b_copies, z_copies = ([], [], [])
    for unit, (chunk, _) in enumerate(units):
        rows = rows_of(unit)
        if chunk % 2 == 0:
            source = products.at[chunk, 1, :, rows, :]
            first_mate, second_mate = (x_mate, y_mate)
        else:
            source = products.at[chunk, :, 1, rows, :]
            first_mate, second_mate = (y_mate, x_mate)
        a_copies.append(copy(source, a_recv.at[unit], a_sems, (unit,), first_mate))
        b_copies.append(copy(b_send.at[unit], b_recv.at[unit], b_sems, (unit,), second_mate))
        z_copies.append(
            [
                copy(
                    z_send.at[unit, z_spots[shift]],
                    z_recv.at[unit, shift],
                    z_sems,
                    (unit, shift),
                    z_mates[shift],
                )
                for shift in range(3)
            ]
        )

    def finish(unit):
        chunk, _ = units[unit]
        b_copies[unit].wait_recv()
        total = (
            products[chunk, 0, 0, rows_of(unit), :].astype(jnp.float32)
            + a_recv[unit, 0].astype(jnp.float32)
            + b_recv[unit].astype(jnp.float32)
        ).astype(jnp.bfloat16)
        for spot in range(4):
            z_send[unit, spot] = total[:, spot * SECOND : (spot + 1) * SECOND]
        for sent in z_copies[unit]:
            sent.start()

    count = len(units)
    ahead = 4
    for unit in range(ahead):
        a_copies[unit].start()
    for unit, (chunk, _) in enumerate(units):
        a_copies[unit].wait_recv()
        side = (0, 1) if chunk % 2 == 0 else (1, 0)
        b_send[unit] = (
            products[chunk, side[0], side[1], rows_of(unit), :].astype(jnp.float32)
            + a_recv[unit, 1].astype(jnp.float32)
        ).astype(jnp.bfloat16)
        b_copies[unit].start()
        if unit + ahead < count:
            a_copies[unit + ahead].start()
        if unit >= 2:
            finish(unit - 2)
    finish(count - 2)
    finish(count - 1)
    for unit, (chunk, _) in enumerate(units):
        total = z_send[unit, z_spot].astype(jnp.float32)
        for shift in range(3):
            z_copies[unit][shift].wait_recv()
            total += z_recv[unit, shift].astype(jnp.float32)
        result[rows_of(unit), chunk * SECOND : (chunk + 1) * SECOND] = total
    for unit in range(count):
        a_copies[unit].wait_send()
        b_copies[unit].wait_send()
        for sent in z_copies[unit]:
            sent.wait_send()


def reduce_products(products):
    chunks, _, _, patch_len, columns = products.shape
    count, height = (2 * chunks, patch_len // 2)
    held = jnp.bfloat16
    return pl.pallas_call(
        reduce_kernel,
        in_specs=[pl.BlockSpec(memory_space=pltpu.VMEM)],
        out_specs=pl.BlockSpec(memory_space=pltpu.VMEM),
        out_shape=jax.ShapeDtypeStruct((patch_len, chunks * SECOND), jnp.float32),
        scratch_shapes=[
            pltpu.VMEM((count, 2, height, columns), held),
            pltpu.VMEM((count, height, columns), held),
            pltpu.VMEM((count, height, columns), held),
            pltpu.VMEM((count, 4, height, SECOND), held),
            pltpu.VMEM((count, 3, height, SECOND), held),
            pltpu.SemaphoreType.DMA((2, count)),
            pltpu.SemaphoreType.DMA((2, count)),
            pltpu.SemaphoreType.DMA((2, count, 3)),
        ],
        compiler_params=pltpu.CompilerParams(
            collective_id=0, has_side_effects=True, vmem_limit_bytes=40 * 1024 * 1024
        ),
    )(products)


def reduced_patch(white_noise, row_start, geometry):
    row_count = lax.axis_size("row")
    patch_len = row_count * ROWS_DEV
    row = lax.axis_index("row")
    over_core = [(r, r ^ 1) for r in range(row_count)]
    host = host_tables()
    kept, moved = half_screens(white_noise, row_start, row, host)
    other_bin = lax.ppermute(geometry[0, 1], "dir", [(0, 1), (1, 0)])
    other_bin, moved = lax.optimization_barrier((other_bin, moved))
    received = lax.ppermute(moved, "row", over_core)
    first_block = 2 * (lax.axis_index("dir") * row_count + row)
    other_block = 2 * (lax.axis_index("dir") * row_count + (row ^ 1))
    block_ids = jnp.stack([first_block, first_block + 1, other_block, other_block + 1])
    slant_bins = jnp.stack([geometry[0, 1], other_bin])
    matrix = patch_matrix(slant_bins, block_ids, patch_len // SECOND, host[3])
    return reduce_products(patch_products(matrix, kept, received))


def turn_kernel(field, result, landed, local_sem, sems):
    here_dir, row = (lax.axis_index("dir"), lax.axis_index("row"))
    count = lax.axis_size("row")
    height = result.shape[1]
    columns = field.shape[2]
    mates = [(here_dir, (row + shift) % count) for shift in range(1, count)]
    barrier = pltpu.get_barrier_semaphore()
    for mate in mates:
        pl.semaphore_signal(barrier, inc=1, device_id=mate, device_id_type=pl.DeviceIdType.MESH)
    pl.semaphore_wait(barrier, len(mates))
    mine = pl.ds(pl.multiple_of(row * columns, columns), columns)

    def rows_of(spot):
        return pl.ds(pl.multiple_of(spot * height, height), height)

    copies = [
        pltpu.make_async_remote_copy(
            src_ref=field.at[:, rows_of(mate[1]), :],
            dst_ref=landed.at[:, :, mine],
            send_sem=sems.at[0, spot],
            recv_sem=sems.at[1, spot],
            device_id=mate,
            device_id_type=pl.DeviceIdType.MESH,
        )
        for spot, mate in enumerate(mates)
    ]
    for sent in copies:
        sent.start()
    local = pltpu.make_async_copy(field.at[:, rows_of(row), :], landed.at[:, :, mine], local_sem)
    local.start()
    local.wait()
    for sent in copies:
        sent.wait_recv()
    result[...] = landed[...]
    for sent in copies:
        sent.wait_send()


def turn_field(field):
    count = lax.axis_size("row")
    parts, patch_len, columns = field.shape
    shape = (parts, patch_len // count, count * columns)
    return pl.pallas_call(
        turn_kernel,
        in_specs=[pl.BlockSpec(memory_space=pltpu.VMEM)],
        out_specs=pl.BlockSpec(memory_space=pltpu.VMEM),
        out_shape=jax.ShapeDtypeStruct(shape, field.dtype),
        scratch_shapes=[
            pltpu.VMEM(shape, field.dtype),
            pltpu.SemaphoreType.DMA,
            pltpu.SemaphoreType.DMA((2, count - 1)),
        ],
        compiler_params=pltpu.CompilerParams(
            collective_id=1, has_side_effects=True, vmem_limit_bytes=16 * 1024 * 1024
        ),
    )(field)


def share_kernel(terms, result, landed, sems):
    rows = lax.axis_size("row")
    count = rows * lax.axis_size("dir")
    here = lax.axis_index("dir") * rows + lax.axis_index("row")
    spots = [(here + shift) % count for shift in range(1, count)]
    mates = [(spot // rows, spot % rows) for spot in spots]
    barrier = pltpu.get_barrier_semaphore()
    for mate in mates:
        pl.semaphore_signal(barrier, inc=1, device_id=mate, device_id_type=pl.DeviceIdType.MESH)
    pl.semaphore_wait(barrier, len(mates))
    copies = [
        pltpu.make_async_remote_copy(
            src_ref=terms.at[spot],
            dst_ref=landed.at[place],
            send_sem=sems.at[0, place],
            recv_sem=sems.at[1, place],
            device_id=mate,
            device_id_type=pl.DeviceIdType.MESH,
        )
        for place, (spot, mate) in enumerate(zip(spots, mates))
    ]
    for sent in copies:
        sent.start()
    total = terms[here]
    for place, sent in enumerate(copies):
        sent.wait_recv()
        total += landed[place]
    result[...] = total
    for sent in copies:
        sent.wait_send()


def share_sums(terms):
    count = terms.shape[0]
    return pl.pallas_call(
        share_kernel,
        in_specs=[pl.BlockSpec(memory_space=pltpu.VMEM)],
        out_specs=pl.BlockSpec(memory_space=pltpu.VMEM),
        out_shape=jax.ShapeDtypeStruct(terms.shape[1:], terms.dtype),
        scratch_shapes=[
            pltpu.VMEM((count - 1, *terms.shape[1:]), terms.dtype),
            pltpu.SemaphoreType.DMA((2, count - 1)),
        ],
        compiler_params=pltpu.CompilerParams(collective_id=2, has_side_effects=True),
    )(terms)


def body(white_noise, geometry, window, tile_map, link_gain, serving):
    row_count = lax.axis_size("row")
    tables = transform_tables(FIRST, SECOND)
    tables_y = transform_tables(row_count, ROWS_DEV)
    patch_len = row_count * ROWS_DEV
    rows_here = white_noise.shape[1]
    row_start = lax.axis_index(("dir", "row")) * rows_here
    slant_factor = 1.0 + 0.25 * geometry[0, 1].astype(jnp.float32)
    fresnel_x = fresnel_factor(geometry[0], FIRST, SECOND)
    fresnel_y = fresnel_factor(geometry[0], row_count, ROWS_DEV)
    direct = lax.axis_size("dir") == 2 and row_count == 16 and rows_here == 2 * SECOND
    if direct:
        phase_patch = reduced_patch(white_noise, row_start, geometry)
    else:
        half_screen = half_screen_rows(white_noise, row_start, tables)
        phase_patch = gathered_patch(half_screen, geometry, tables, patch_len)
    columns = phase_patch.shape[1]
    screen_field = propagate_columns(phase_patch, tables_y, slant_factor, fresnel_y)
    if direct:
        portion = turn_field(screen_field)[:, None]
    else:
        stacked_field = screen_field.reshape(2, row_count, ROWS_DEV, columns)
        portion = lax.all_to_all(stacked_field, "row", split_axis=1, concat_axis=3, tiled=True)
    item_count = portion.shape[2]
    stacked = portion.reshape(2, item_count, FIRST, SECOND)
    spectral = forward_axis(stacked, tables, fresnel_x, row_patterns, False)
    wave_field = inverse_axis(spectral, tables, row_patterns, False)
    intensity = wave_field[0] * wave_field[0] + wave_field[1] * wave_field[1]
    intensity = intensity.reshape(item_count, XTILES, TILE_X)
    tile_one = jnp.sum(intensity, axis=2)
    tile_two = jnp.sum(intensity * intensity, axis=2)
    tile_rows = ROWS_DEV // YTILES
    first_moment = jnp.sum(tile_one.reshape(YTILES, tile_rows, XTILES), axis=1)
    second_moment = jnp.sum(tile_two.reshape(YTILES, tile_rows, XTILES), axis=1)
    fluctuation, faded_power = tile_statistics(first_moment, second_moment, window[0], tile_rows)
    faded_flat = faded_power.reshape(-1)
    tile_total = faded_flat.shape[0]
    local_tile = tile_map[0] - lax.axis_index("row") * tile_total
    inside = (local_tile >= 0) & (local_tile < tile_total)
    looked = jnp.where(inside, jnp.take(faded_flat, jnp.clip(local_tile, 0, tile_total - 1)), 0.0)
    received = link_gain[0] * looked
    direction = lax.axis_index("dir")
    serves_here = serving == direction
    signal_part = jnp.where(serves_here, received, 0.0)
    interference_part = jnp.where(serves_here, 0.0, received)
    device_count = lax.axis_size(("dir", "row"))
    terms = jnp.stack([signal_part, interference_part]).reshape(2, device_count, -1)
    if direct:
        share = terms.shape[2]
        padded = jnp.pad(
            terms.transpose(1, 0, 2).reshape(device_count, 1, 2 * share),
            ((0, 0), (0, 0), (0, SECOND - 2 * share)),
        )
        summed = share_sums(padded)[0]
        signal, interference = (summed[:share], summed[share : 2 * share])
    else:
        gathered = lax.all_to_all(
            terms.transpose(1, 0, 2), ("dir", "row"), split_axis=0, concat_axis=0, tiled=True
        )
        signal, interference = jnp.sum(gathered, axis=0)
    signal_ratio = jnp.log10(signal / (interference + noise_floor))
    return (fluctuation[None], signal_ratio)


def solution(mesh):
    return jax.shard_map(
        body,
        mesh=mesh,
        in_specs=(
            P(None, ("dir", "row"), None),
            P("dir", None),
            P("dir"),
            P("dir", None),
            P("dir", None),
            P(),
        ),
        out_specs=(P("dir", "row", None), P(("dir", "row"))),
        check_vma=False,
    )
```

```python
import math

import jax
import jax.numpy as jnp
import ml_dtypes
import numpy as np
from jax import lax
from jax.experimental import pallas as pl
from jax.experimental.pallas import tpu as pltpu
from jax.sharding import PartitionSpec as P

N = 8192
FIRST = 64
SECOND = 128
ROWS_DEV = 32
XTILES = 128
YTILES = 8
TILE_X = 64
GROUP = 8
CHUNKS = 4


full_turn = 2.0 * math.pi
noise_floor = 0.05
tiny_value = 1e-06
strength = 1.6
row_patterns = (
    "zrab,zwak->wrkb",
    "zrkb,zwbc->wrkc",
    "zrkc,wzbc->wrkb",
    "zrkb,wzak->wrab",
    "zrkb,zak->rab",
)
column_patterns = (
    "zaby,zwak->wkby",
    "zkby,zwbc->wkcy",
    "zkcy,wzbc->wkby",
    "zkby,wzak->waby",
    "zkby,zak->aby",
)


def complex_block(real_part, imag_part):
    return jnp.stack(
        [jnp.stack([real_part, imag_part]), jnp.stack([-imag_part, real_part])]
    ).astype(jnp.bfloat16)


def transform_tables(first, second):
    total = first * second
    outer_ids = jnp.arange(first, dtype=jnp.int32)
    inner_ids = jnp.arange(second, dtype=jnp.int32)
    outer_angle = (outer_ids[:, None] * outer_ids[None, :] % first).astype(jnp.float32) * (
        full_turn / first
    )
    inner_angle = (inner_ids[:, None] * inner_ids[None, :] % second).astype(jnp.float32) * (
        full_turn / second
    )
    twist_angle = (outer_ids[:, None] * inner_ids[None, :] % total).astype(jnp.float32) * (
        full_turn / total
    )
    return (
        complex_block(jnp.cos(outer_angle), -jnp.sin(outer_angle)),
        complex_block(jnp.cos(inner_angle), -jnp.sin(inner_angle)),
        jnp.cos(twist_angle),
        -jnp.sin(twist_angle),
    )


def signed_wave(positions, first, second):
    total = first * second
    wave_number = positions // second + first * (positions % second)
    return jnp.where(wave_number >= total // 2, wave_number - total, wave_number).astype(
        jnp.float32
    )


def spectral_filter(row_ids, column_ids):
    wave_rows = signed_wave(row_ids, FIRST, SECOND)
    wave_columns = signed_wave(column_ids, FIRST, SECOND)
    squared_radius = 16.0 + wave_rows[:, None] ** 2 + wave_columns[None, :] ** 2
    return strength * float(N) * float(N) * squared_radius ** (-0.75)


def fresnel_factor(geometry_row, first, second):
    total = first * second
    fresnel_area = 144.0 * jnp.exp2(geometry_row[0].astype(jnp.float32))
    positions = jnp.arange(total, dtype=jnp.int32).reshape(first, second)
    scaled = signed_wave(positions, first, second) * (full_turn / total)
    turning = 0.5 * scaled * scaled * fresnel_area
    return (jnp.cos(turning), -jnp.sin(turning))


def complex_times(values, real_part, imag_part):
    return jnp.stack(
        [
            values[0] * real_part - values[1] * imag_part,
            values[0] * imag_part + values[1] * real_part,
        ]
    )


def contract(pattern, operand, matrix):
    return jnp.einsum(pattern, operand, matrix, preferred_element_type=jnp.float32)


def table_length(tables):
    return tables[0].shape[2] * tables[1].shape[2]


def forward_axis(values, tables, factor, patterns, trailing):
    outer_table, inner_table, twist_real, twist_imag = tables
    factor_real, factor_imag = factor
    if trailing:
        twist_real, twist_imag = (twist_real[..., None], twist_imag[..., None])
        factor_real, factor_imag = (factor_real[..., None], factor_imag[..., None])
    section_one = complex_times(
        contract(patterns[0], values, outer_table), twist_real, twist_imag
    ).astype(jnp.bfloat16)
    section_two = contract(patterns[1], section_one, inner_table)
    return complex_times(section_two, factor_real, factor_imag).astype(jnp.bfloat16)


def inverse_first(values, tables, patterns, trailing):
    outer_table, inner_table, twist_real, twist_imag = tables
    if trailing:
        twist_real, twist_imag = (twist_real[..., None], twist_imag[..., None])
    return complex_times(
        contract(patterns[2], values, inner_table), twist_real, -twist_imag
    ).astype(jnp.bfloat16)


def inverse_axis(values, tables, patterns, trailing):
    section_one = inverse_first(values, tables, patterns, trailing)
    return contract(patterns[3], section_one, tables[0]) * (1.0 / table_length(tables))


def window_matrix(half_width):
    positions = jnp.arange(XTILES, dtype=jnp.int32)
    difference = (positions[:, None] - positions[None, :]) % XTILES
    distance = jnp.minimum(difference, XTILES - difference)
    return (distance <= half_width).astype(jnp.float32)


def tile_statistics(first_moment, second_moment, half_width, tile_rows):
    window_mask = window_matrix(half_width)
    cells = ((2 * half_width + 1) * (TILE_X * tile_rows)).astype(jnp.float32)
    mean_one = jnp.dot(first_moment, window_mask, precision=lax.Precision.HIGHEST) / cells
    mean_two = jnp.dot(second_moment, window_mask, precision=lax.Precision.HIGHEST) / cells
    fluctuation = mean_two / (mean_one * mean_one + tiny_value) - 1.0
    return (fluctuation, mean_one * jnp.exp(-fluctuation))


def propagate_columns(phase_patch, tables_y, slant_factor, fresnel_y):
    patch_rows = phase_patch.shape[0]
    width_here = phase_patch.shape[1]
    outer_len = tables_y[0].shape[2]
    inner_len = tables_y[1].shape[2]
    turned_phase = slant_factor * phase_patch
    screen_field = jnp.stack([jnp.cos(turned_phase), jnp.sin(turned_phase)]).astype(jnp.bfloat16)
    stacked = screen_field.reshape(2, outer_len, inner_len, width_here)
    spectral = forward_axis(stacked, tables_y, fresnel_y, column_patterns, True)
    result = inverse_axis(spectral, tables_y, column_patterns, True)
    return result.astype(jnp.bfloat16).reshape(2, patch_rows, width_here)


def half_screen_rows(white_noise, row_start, tables):
    rows_here = white_noise.shape[1]
    row_ids = row_start + jnp.arange(rows_here, dtype=jnp.int32)
    column_ids = jnp.arange(N, dtype=jnp.int32)
    spectral_gain = spectral_filter(row_ids, column_ids)
    spectrum = (white_noise.astype(jnp.float32) * spectral_gain).astype(jnp.bfloat16)
    half_screen = inverse_axis(
        spectrum.reshape(2, rows_here, FIRST, SECOND), tables, row_patterns, False
    )
    half_screen = half_screen.astype(jnp.bfloat16).reshape(2, rows_here, N)
    return half_screen


def gathered_patch(half_screen, geometry, tables, patch_len):
    turned = lax.all_to_all(half_screen, "row", split_axis=2, concat_axis=1, tiled=True)
    band_rows = turned.shape[1]
    columns = turned.shape[2]
    offset_rows = N // 4 * geometry[0, 1]
    blocks = band_rows // SECOND
    block_start = lax.axis_index("dir") * blocks
    stacked = turned.reshape(2, blocks, SECOND, columns)
    twist_real = lax.dynamic_slice_in_dim(tables[2], block_start, blocks, 0)[..., None]
    twist_imag = lax.dynamic_slice_in_dim(tables[3], block_start, blocks, 0)[..., None]
    section_one = complex_times(
        contract("zkcx,wzbc->wkbx", stacked, tables[1]), twist_real, -twist_imag
    )
    section_one = section_one.astype(jnp.bfloat16)
    outer_count = patch_len // SECOND
    outer_ids = (offset_rows // SECOND + jnp.arange(outer_count, dtype=jnp.int32)) % FIRST
    patch_outer = jnp.take(tables[0][0], outer_ids, axis=1)
    phase_patch = contract(
        "zkbx,zak->abx", lax.all_gather(section_one, "dir", axis=1, tiled=True), patch_outer
    )
    return phase_patch.reshape(patch_len, columns) * (1.0 / N)


def host_tables():
    def block(length):
        ids = np.arange(length)
        angle = (ids[:, None] * ids[None, :] % length) * (full_turn / length)
        real_part, imag_part = (np.cos(angle), np.sin(angle))
        return np.array([[real_part, -imag_part], [imag_part, real_part]])

    inner = block(SECOND).transpose(1, 3, 0, 2).reshape(2 * SECOND, 2 * SECOND)
    outer = block(FIRST).transpose(0, 2, 1, 3).reshape(2 * FIRST, 2 * FIRST)
    spread = np.kron(outer, np.eye(GROUP))
    twist = np.arange(FIRST)[:, None] * np.arange(SECOND)[None, :] * (full_turn / N)
    twist = np.repeat(twist, GROUP, axis=0)
    angle = (np.arange(SECOND)[:, None] * np.arange(SECOND)[None, :] % SECOND) * (full_turn / SECOND)
    return (
        inner.astype(ml_dtypes.bfloat16),
        np.stack([np.cos(twist), np.sin(twist)]).astype(np.float32),
        spread.astype(ml_dtypes.bfloat16),
        np.stack([np.cos(angle), np.sin(angle)]).astype(np.float32),
    )


def screen_kernel(
    spot, noise, rows_squared, columns_squared, inner, twist, spread, kept, moved, staged
):
    core, y_spot = (spot[0], spot[1])
    root = lax.rsqrt(16.0 + rows_squared[...] + columns_squared[...])
    gain = strength * root * (root * lax.rsqrt(root))
    spectrum = [noise[z].astype(jnp.float32) * gain for z in range(2)]
    sections = []
    for group in range(2):
        rows = slice(group * GROUP, (group + 1) * GROUP)
        parts = [
            jnp.concatenate(
                [spectrum[z][rows, k * SECOND : (k + 1) * SECOND] for k in range(FIRST)], axis=0
            ).astype(jnp.bfloat16)
            for z in range(2)
        ]
        first = jnp.dot(
            jnp.concatenate(parts, axis=1), inner[...], preferred_element_type=jnp.float32
        )
        real_part, imag_part = (first[:, :SECOND], first[:, SECOND:])
        turned = jnp.concatenate(
            [
                real_part * twist[0] - imag_part * twist[1],
                real_part * twist[1] + imag_part * twist[0],
            ],
            axis=0,
        )
        sections.append(turned.astype(jnp.bfloat16))
    staged[...] = jnp.dot(
        spread[...], jnp.concatenate(sections, axis=1), preferred_element_type=jnp.float32
    )
    for core_side, target in enumerate((kept, moved)):
        for y_side in range(2):
            for chunk in range(CHUNKS):
                for z_spot in range(4):
                    place = z_spot * 4 + (y_spot ^ y_side) * 2 + (core ^ core_side)
                    for w in range(2):
                        start = (w * FIRST + place * CHUNKS + chunk) * GROUP
                        taken = staged[pl.ds(pl.multiple_of(start, GROUP), GROUP), :]
                        both = jnp.concatenate([taken[:, :SECOND], taken[:, SECOND:]], axis=0)
                        target[y_side, chunk, w, :, z_spot * SECOND : (z_spot + 1) * SECOND] = (
                            both.astype(jnp.bfloat16)
                        )


def half_screens(white_noise, row_start, row, host):
    rows_here = white_noise.shape[1]
    inner, twist, spread, _ = host
    row_waves = signed_wave(row_start + jnp.arange(rows_here, dtype=jnp.int32), FIRST, SECOND)
    column_waves = signed_wave(jnp.arange(N, dtype=jnp.int32), FIRST, SECOND)
    spot = jnp.stack([row % 2, row // 2 % 2])
    step = 2 * GROUP
    out_shape = (2, CHUNKS, 2, rows_here, 4 * SECOND)
    out_spec = pl.BlockSpec((2, CHUNKS, 2, step, 4 * SECOND), lambda i: (0, 0, 0, i, 0))

    def whole(array):
        return pl.BlockSpec(array.shape, lambda i: (0,) * array.ndim)

    return pl.pallas_call(
        screen_kernel,
        grid=(rows_here // step,),
        in_specs=[
            pl.BlockSpec(memory_space=pltpu.SMEM),
            pl.BlockSpec((2, step, N), lambda i: (0, i, 0)),
            pl.BlockSpec((step, 1), lambda i: (i, 0)),
            pl.BlockSpec((1, N), lambda i: (0, 0)),
            whole(inner),
            whole(twist),
            whole(spread),
        ],
        out_specs=[out_spec, out_spec],
        out_shape=[jax.ShapeDtypeStruct(out_shape, jnp.bfloat16)] * 2,
        scratch_shapes=[pltpu.VMEM((2 * FIRST * GROUP, 2 * SECOND), jnp.float32)],
        compiler_params=pltpu.CompilerParams(vmem_limit_bytes=48 * 1024 * 1024),
        cost_estimate=pl.CostEstimate(
            flops=20_000_000_000, bytes_accessed=20_000_000, transcendentals=4_000_000
        ),
    )(
        spot,
        white_noise,
        (row_waves * row_waves)[:, None],
        (column_waves * column_waves)[None, :],
        inner,
        twist,
        spread,
    )


def matrix_kernel(slow, fast, matrix):
    for outer in range(matrix.shape[0] // SECOND):
        rows = slice(outer * SECOND, (outer + 1) * SECOND)
        for source in range(2):
            for near in range(2):
                block = source * 2 + near
                slow_real = slow[0, rows, block : block + 1]
                slow_imag = slow[1, rows, block : block + 1]
                real_part = slow_real * fast[0] - slow_imag * fast[1]
                imag_part = slow_real * fast[1] + slow_imag * fast[0]
                for z, part in enumerate((real_part, -imag_part)):
                    start = ((source * 2 + z) * 2 + near) * SECOND
                    matrix[rows, start : start + SECOND] = part.astype(jnp.bfloat16)


def patch_matrix(slant_bins, block_ids, outer_count, fast):
    inner_ids = jnp.arange(SECOND, dtype=jnp.int32)
    outer_ids = slant_bins[:, None] * (FIRST // 4) + jnp.arange(outer_count, dtype=jnp.int32)
    position = (outer_ids[:, :, None] * SECOND + inner_ids).reshape(-1)
    slow = (position[:, None] * block_ids[None, :] % N).astype(jnp.float32) * (full_turn / N)
    slow = jnp.stack([jnp.cos(slow), jnp.sin(slow)])
    length = position.shape[0]
    return pl.pallas_call(
        matrix_kernel,
        grid=(2,),
        in_specs=[
            pl.BlockSpec((2, length // 2, 4), lambda i: (0, i, 0)),
            pl.BlockSpec(fast.shape, lambda i: (0, 0, 0)),
        ],
        out_specs=pl.BlockSpec((length // 2, 8 * SECOND), lambda i: (i, 0)),
        out_shape=jax.ShapeDtypeStruct((length, 8 * SECOND), jnp.bfloat16),
        cost_estimate=pl.CostEstimate(
            flops=8_000_000, bytes_accessed=4_000_000, transcendentals=0
        ),
    )(slow, fast)


def product_kernel(matrix, kept, received, result):
    depth = kept.shape[0] * kept.shape[1]
    columns = kept.shape[2]
    total = jnp.dot(
        matrix[:, :depth],
        kept[...].reshape(depth, columns),
        preferred_element_type=jnp.float32,
    )
    total += jnp.dot(
        matrix[:, depth:],
        received[...].reshape(depth, columns),
        preferred_element_type=jnp.float32,
    )
    result[...] = total.astype(result.dtype).reshape(result.shape)


def patch_products(matrix, kept, received):
    patch_len = matrix.shape[0] // 2
    sides, chunks, parts, rows, columns = kept.shape
    values_spec = pl.BlockSpec(
        (None, None, parts, rows, columns), lambda i, j: (j, i, 0, 0, 0)
    )
    return pl.pallas_call(
        product_kernel,
        grid=(chunks, sides),
        in_specs=[
            pl.BlockSpec(matrix.shape, lambda i, j: (0, 0)),
            values_spec,
            values_spec,
        ],
        out_specs=pl.BlockSpec(
            (None, 2, None, patch_len, columns), lambda i, j: (i, 0, j, 0, 0)
        ),
        out_shape=jax.ShapeDtypeStruct((chunks, 2, sides, patch_len, columns), jnp.bfloat16),
        compiler_params=pltpu.CompilerParams(vmem_limit_bytes=32 * 1024 * 1024),
        cost_estimate=pl.CostEstimate(
            flops=9_000_000_000, bytes_accessed=20_000_000, transcendentals=0
        ),
    )(matrix, kept, received)


def reduce_kernel(
    products, result, a_recv, b_send, b_recv, z_send, z_recv, a_sems, b_sems, z_sems
):
    here_x, row = (lax.axis_index("dir"), lax.axis_index("row"))
    z_spot, y_spot = (row // 4, row // 2 % 2)
    x_mate = (1 - here_x, row)
    y_mate = (here_x, row + 2 - 4 * y_spot)
    z_spots = [(z_spot + shift) % 4 for shift in range(1, 4)]
    z_mates = [(here_x, row + 4 * (spot - z_spot)) for spot in z_spots]
    mates = [x_mate, y_mate] + z_mates
    barrier = pltpu.get_barrier_semaphore()
    for mate in mates:
        pl.semaphore_signal(barrier, inc=1, device_id=mate, device_id_type=pl.DeviceIdType.MESH)
    pl.semaphore_wait(barrier, len(mates))

    height = a_recv.shape[2]
    units = [
        (2 * pair + way, half) for pair in range(2) for half in range(2) for way in range(2)
    ]

    def copy(source, target, sems, spot, mate):
        return pltpu.make_async_remote_copy(
            src_ref=source,
            dst_ref=target,
            send_sem=sems.at[(0, *spot)],
            recv_sem=sems.at[(1, *spot)],
            device_id=mate,
            device_id_type=pl.DeviceIdType.MESH,
        )

    def rows_of(unit):
        return pl.ds(units[unit][1] * height, height)

    a_copies, b_copies, z_copies = ([], [], [])
    for unit, (chunk, _) in enumerate(units):
        rows = rows_of(unit)
        if chunk % 2 == 0:
            source = products.at[chunk, 1, :, rows, :]
            first_mate, second_mate = (x_mate, y_mate)
        else:
            source = products.at[chunk, :, 1, rows, :]
            first_mate, second_mate = (y_mate, x_mate)
        a_copies.append(copy(source, a_recv.at[unit], a_sems, (unit,), first_mate))
        b_copies.append(copy(b_send.at[unit], b_recv.at[unit], b_sems, (unit,), second_mate))
        z_copies.append(
            [
                copy(
                    z_send.at[unit, z_spots[shift]],
                    z_recv.at[unit, shift],
                    z_sems,
                    (unit, shift),
                    z_mates[shift],
                )
                for shift in range(3)
            ]
        )

    def finish(unit):
        chunk, _ = units[unit]
        b_copies[unit].wait_recv()
        total = (
            products[chunk, 0, 0, rows_of(unit), :].astype(jnp.float32)
            + a_recv[unit, 0].astype(jnp.float32)
            + b_recv[unit].astype(jnp.float32)
        ).astype(jnp.bfloat16)
        for spot in range(4):
            z_send[unit, spot] = total[:, spot * SECOND : (spot + 1) * SECOND]
        for sent in z_copies[unit]:
            sent.start()

    count = len(units)
    ahead = 2
    for unit in range(ahead):
        a_copies[unit].start()
    for unit, (chunk, _) in enumerate(units):
        if unit >= 2:
            finish(unit - 2)
        a_copies[unit].wait_recv()
        side = (0, 1) if chunk % 2 == 0 else (1, 0)
        b_send[unit] = (
            products[chunk, side[0], side[1], rows_of(unit), :].astype(jnp.float32)
            + a_recv[unit, 1].astype(jnp.float32)
        ).astype(jnp.bfloat16)
        b_copies[unit].start()
        if unit + ahead < count:
            a_copies[unit + ahead].start()
    finish(count - 2)
    finish(count - 1)
    for unit, (chunk, _) in enumerate(units):
        total = z_send[unit, z_spot].astype(jnp.float32)
        for shift in range(3):
            z_copies[unit][shift].wait_recv()
            total += z_recv[unit, shift].astype(jnp.float32)
        result[rows_of(unit), chunk * SECOND : (chunk + 1) * SECOND] = total
    for unit in range(count):
        a_copies[unit].wait_send()
        b_copies[unit].wait_send()
        for sent in z_copies[unit]:
            sent.wait_send()


def reduce_products(products):
    chunks, _, _, patch_len, columns = products.shape
    count, height = (2 * chunks, patch_len // 2)
    held = jnp.bfloat16
    return pl.pallas_call(
        reduce_kernel,
        in_specs=[pl.BlockSpec(memory_space=pltpu.VMEM)],
        out_specs=pl.BlockSpec(memory_space=pltpu.VMEM),
        out_shape=jax.ShapeDtypeStruct((patch_len, chunks * SECOND), jnp.float32),
        scratch_shapes=[
            pltpu.VMEM((count, 2, height, columns), held),
            pltpu.VMEM((count, height, columns), held),
            pltpu.VMEM((count, height, columns), held),
            pltpu.VMEM((count, 4, height, SECOND), held),
            pltpu.VMEM((count, 3, height, SECOND), held),
            pltpu.SemaphoreType.DMA((2, count)),
            pltpu.SemaphoreType.DMA((2, count)),
            pltpu.SemaphoreType.DMA((2, count, 3)),
        ],
        compiler_params=pltpu.CompilerParams(
            collective_id=0, has_side_effects=True, vmem_limit_bytes=40 * 1024 * 1024
        ),
    )(products)


def reduced_patch(white_noise, row_start, geometry):
    row_count = lax.axis_size("row")
    patch_len = row_count * ROWS_DEV
    row = lax.axis_index("row")
    over_core = [(r, r ^ 1) for r in range(row_count)]
    host = host_tables()
    kept, moved = half_screens(white_noise, row_start, row, host)
    received = lax.ppermute(moved, "row", over_core)
    slant_bin, kept = lax.optimization_barrier((geometry[0, 1], kept))
    other_bin = lax.ppermute(slant_bin, "dir", [(0, 1), (1, 0)])
    first_block = 2 * (lax.axis_index("dir") * row_count + row)
    other_block = 2 * (lax.axis_index("dir") * row_count + (row ^ 1))
    block_ids = jnp.stack([first_block, first_block + 1, other_block, other_block + 1])
    slant_bins = jnp.stack([slant_bin, other_bin])
    matrix = patch_matrix(slant_bins, block_ids, patch_len // SECOND, host[3])
    return reduce_products(patch_products(matrix, kept, received))


def turn_kernel(field, result, landed, local_sem, sems):
    here_dir, row = (lax.axis_index("dir"), lax.axis_index("row"))
    count = lax.axis_size("row")
    height = result.shape[1]
    columns = field.shape[2]
    mates = [(here_dir, (row + shift) % count) for shift in range(1, count)]
    barrier = pltpu.get_barrier_semaphore()
    for mate in mates:
        pl.semaphore_signal(barrier, inc=1, device_id=mate, device_id_type=pl.DeviceIdType.MESH)
    pl.semaphore_wait(barrier, len(mates))
    mine = pl.ds(pl.multiple_of(row * columns, columns), columns)

    def rows_of(spot):
        return pl.ds(pl.multiple_of(spot * height, height), height)

    copies = [
        pltpu.make_async_remote_copy(
            src_ref=field.at[:, rows_of(mate[1]), :],
            dst_ref=landed.at[:, :, mine],
            send_sem=sems.at[0, spot],
            recv_sem=sems.at[1, spot],
            device_id=mate,
            device_id_type=pl.DeviceIdType.MESH,
        )
        for spot, mate in enumerate(mates)
    ]
    for sent in copies:
        sent.start()
    local = pltpu.make_async_copy(field.at[:, rows_of(row), :], landed.at[:, :, mine], local_sem)
    local.start()
    local.wait()
    for sent in copies:
        sent.wait_recv()
    result[...] = landed[...]
    for sent in copies:
        sent.wait_send()


def turn_field(field):
    count = lax.axis_size("row")
    parts, patch_len, columns = field.shape
    shape = (parts, patch_len // count, count * columns)
    return pl.pallas_call(
        turn_kernel,
        in_specs=[pl.BlockSpec(memory_space=pltpu.VMEM)],
        out_specs=pl.BlockSpec(memory_space=pltpu.VMEM),
        out_shape=jax.ShapeDtypeStruct(shape, field.dtype),
        scratch_shapes=[
            pltpu.VMEM(shape, field.dtype),
            pltpu.SemaphoreType.DMA,
            pltpu.SemaphoreType.DMA((2, count - 1)),
        ],
        compiler_params=pltpu.CompilerParams(
            collective_id=1, has_side_effects=True, vmem_limit_bytes=16 * 1024 * 1024
        ),
    )(field)


def share_kernel(terms, result, landed, sems):
    rows = lax.axis_size("row")
    count = rows * lax.axis_size("dir")
    here = lax.axis_index("dir") * rows + lax.axis_index("row")
    spots = [(here + shift) % count for shift in range(1, count)]
    mates = [(spot // rows, spot % rows) for spot in spots]
    barrier = pltpu.get_barrier_semaphore()
    for mate in mates:
        pl.semaphore_signal(barrier, inc=1, device_id=mate, device_id_type=pl.DeviceIdType.MESH)
    pl.semaphore_wait(barrier, len(mates))
    copies = [
        pltpu.make_async_remote_copy(
            src_ref=terms.at[spot],
            dst_ref=landed.at[place],
            send_sem=sems.at[0, place],
            recv_sem=sems.at[1, place],
            device_id=mate,
            device_id_type=pl.DeviceIdType.MESH,
        )
        for place, (spot, mate) in enumerate(zip(spots, mates))
    ]
    for sent in copies:
        sent.start()
    total = terms[here]
    for place, sent in enumerate(copies):
        sent.wait_recv()
        total += landed[place]
    result[...] = total
    for sent in copies:
        sent.wait_send()


def share_sums(terms):
    count = terms.shape[0]
    return pl.pallas_call(
        share_kernel,
        in_specs=[pl.BlockSpec(memory_space=pltpu.VMEM)],
        out_specs=pl.BlockSpec(memory_space=pltpu.VMEM),
        out_shape=jax.ShapeDtypeStruct(terms.shape[1:], terms.dtype),
        scratch_shapes=[
            pltpu.VMEM((count - 1, *terms.shape[1:]), terms.dtype),
            pltpu.SemaphoreType.DMA((2, count - 1)),
        ],
        compiler_params=pltpu.CompilerParams(collective_id=2, has_side_effects=True),
    )(terms)


def body(white_noise, geometry, window, tile_map, link_gain, serving):
    row_count = lax.axis_size("row")
    tables = transform_tables(FIRST, SECOND)
    tables_y = transform_tables(row_count, ROWS_DEV)
    patch_len = row_count * ROWS_DEV
    rows_here = white_noise.shape[1]
    row_start = lax.axis_index(("dir", "row")) * rows_here
    slant_factor = 1.0 + 0.25 * geometry[0, 1].astype(jnp.float32)
    fresnel_x = fresnel_factor(geometry[0], FIRST, SECOND)
    fresnel_y = fresnel_factor(geometry[0], row_count, ROWS_DEV)
    direct = lax.axis_size("dir") == 2 and row_count == 16 and rows_here == 2 * SECOND
    if direct:
        phase_patch = reduced_patch(white_noise, row_start, geometry)
    else:
        half_screen = half_screen_rows(white_noise, row_start, tables)
        phase_patch = gathered_patch(half_screen, geometry, tables, patch_len)
    columns = phase_patch.shape[1]
    screen_field = propagate_columns(phase_patch, tables_y, slant_factor, fresnel_y)
    if direct:
        portion = turn_field(screen_field)[:, None]
    else:
        stacked_field = screen_field.reshape(2, row_count, ROWS_DEV, columns)
        portion = lax.all_to_all(stacked_field, "row", split_axis=1, concat_axis=3, tiled=True)
    item_count = portion.shape[2]
    stacked = portion.reshape(2, item_count, FIRST, SECOND)
    spectral = forward_axis(stacked, tables, fresnel_x, row_patterns, False)
    wave_field = inverse_axis(spectral, tables, row_patterns, False)
    intensity = wave_field[0] * wave_field[0] + wave_field[1] * wave_field[1]
    intensity = intensity.reshape(item_count, XTILES, TILE_X)
    tile_one = jnp.sum(intensity, axis=2)
    tile_two = jnp.sum(intensity * intensity, axis=2)
    tile_rows = ROWS_DEV // YTILES
    first_moment = jnp.sum(tile_one.reshape(YTILES, tile_rows, XTILES), axis=1)
    second_moment = jnp.sum(tile_two.reshape(YTILES, tile_rows, XTILES), axis=1)
    fluctuation, faded_power = tile_statistics(first_moment, second_moment, window[0], tile_rows)
    faded_flat = faded_power.reshape(-1)
    tile_total = faded_flat.shape[0]
    local_tile = tile_map[0] - lax.axis_index("row") * tile_total
    inside = (local_tile >= 0) & (local_tile < tile_total)
    looked = jnp.where(inside, jnp.take(faded_flat, jnp.clip(local_tile, 0, tile_total - 1)), 0.0)
    received = link_gain[0] * looked
    direction = lax.axis_index("dir")
    serves_here = serving == direction
    signal_part = jnp.where(serves_here, received, 0.0)
    interference_part = jnp.where(serves_here, 0.0, received)
    device_count = lax.axis_size(("dir", "row"))
    terms = jnp.stack([signal_part, interference_part]).reshape(2, device_count, -1)
    if direct:
        share = terms.shape[2]
        padded = jnp.pad(
            terms.transpose(1, 0, 2).reshape(device_count, 1, 2 * share),
            ((0, 0), (0, 0), (0, SECOND - 2 * share)),
        )
        summed = share_sums(padded)[0]
        signal, interference = (summed[:share], summed[share : 2 * share])
    else:
        gathered = lax.all_to_all(
            terms.transpose(1, 0, 2), ("dir", "row"), split_axis=0, concat_axis=0, tiled=True
        )
        signal, interference = jnp.sum(gathered, axis=0)
    signal_ratio = jnp.log10(signal / (interference + noise_floor))
    return (fluctuation[None], signal_ratio)


def solution(mesh):
    return jax.shard_map(
        body,
        mesh=mesh,
        in_specs=(
            P(None, ("dir", "row"), None),
            P("dir", None),
            P("dir"),
            P("dir", None),
            P("dir", None),
            P(),
        ),
        out_specs=(P("dir", "row", None), P(("dir", "row"))),
        check_vma=False,
    )
```

```python
import math

import jax
import jax.numpy as jnp
import ml_dtypes
import numpy as np
from jax import lax
from jax.experimental import pallas as pl
from jax.experimental.pallas import tpu as pltpu
from jax.sharding import PartitionSpec as P

N = 8192
FIRST = 64
SECOND = 128
ROWS_DEV = 32
XTILES = 128
YTILES = 8
TILE_X = 64
GROUP = 8
CHUNKS = 4


full_turn = 2.0 * math.pi
noise_floor = 0.05
tiny_value = 1e-06
strength = 1.6
row_patterns = (
    "zrab,zwak->wrkb",
    "zrkb,zwbc->wrkc",
    "zrkc,wzbc->wrkb",
    "zrkb,wzak->wrab",
    "zrkb,zak->rab",
)
column_patterns = (
    "zaby,zwak->wkby",
    "zkby,zwbc->wkcy",
    "zkcy,wzbc->wkby",
    "zkby,wzak->waby",
    "zkby,zak->aby",
)


def complex_block(real_part, imag_part):
    return jnp.stack(
        [jnp.stack([real_part, imag_part]), jnp.stack([-imag_part, real_part])]
    ).astype(jnp.bfloat16)


def transform_tables(first, second):
    total = first * second
    outer_ids = jnp.arange(first, dtype=jnp.int32)
    inner_ids = jnp.arange(second, dtype=jnp.int32)
    outer_angle = (outer_ids[:, None] * outer_ids[None, :] % first).astype(jnp.float32) * (
        full_turn / first
    )
    inner_angle = (inner_ids[:, None] * inner_ids[None, :] % second).astype(jnp.float32) * (
        full_turn / second
    )
    twist_angle = (outer_ids[:, None] * inner_ids[None, :] % total).astype(jnp.float32) * (
        full_turn / total
    )
    return (
        complex_block(jnp.cos(outer_angle), -jnp.sin(outer_angle)),
        complex_block(jnp.cos(inner_angle), -jnp.sin(inner_angle)),
        jnp.cos(twist_angle),
        -jnp.sin(twist_angle),
    )


def signed_wave(positions, first, second):
    total = first * second
    wave_number = positions // second + first * (positions % second)
    return jnp.where(wave_number >= total // 2, wave_number - total, wave_number).astype(
        jnp.float32
    )


def spectral_filter(row_ids, column_ids):
    wave_rows = signed_wave(row_ids, FIRST, SECOND)
    wave_columns = signed_wave(column_ids, FIRST, SECOND)
    squared_radius = 16.0 + wave_rows[:, None] ** 2 + wave_columns[None, :] ** 2
    return strength * float(N) * float(N) * squared_radius ** (-0.75)


def fresnel_factor(geometry_row, first, second):
    total = first * second
    fresnel_area = 144.0 * jnp.exp2(geometry_row[0].astype(jnp.float32))
    positions = jnp.arange(total, dtype=jnp.int32).reshape(first, second)
    scaled = signed_wave(positions, first, second) * (full_turn / total)
    turning = 0.5 * scaled * scaled * fresnel_area
    return (jnp.cos(turning), -jnp.sin(turning))


def complex_times(values, real_part, imag_part):
    return jnp.stack(
        [
            values[0] * real_part - values[1] * imag_part,
            values[0] * imag_part + values[1] * real_part,
        ]
    )


def contract(pattern, operand, matrix):
    return jnp.einsum(pattern, operand, matrix, preferred_element_type=jnp.float32)


def table_length(tables):
    return tables[0].shape[2] * tables[1].shape[2]


def forward_axis(values, tables, factor, patterns, trailing):
    outer_table, inner_table, twist_real, twist_imag = tables
    factor_real, factor_imag = factor
    if trailing:
        twist_real, twist_imag = (twist_real[..., None], twist_imag[..., None])
        factor_real, factor_imag = (factor_real[..., None], factor_imag[..., None])
    section_one = complex_times(
        contract(patterns[0], values, outer_table), twist_real, twist_imag
    ).astype(jnp.bfloat16)
    section_two = contract(patterns[1], section_one, inner_table)
    return complex_times(section_two, factor_real, factor_imag).astype(jnp.bfloat16)


def inverse_first(values, tables, patterns, trailing):
    outer_table, inner_table, twist_real, twist_imag = tables
    if trailing:
        twist_real, twist_imag = (twist_real[..., None], twist_imag[..., None])
    return complex_times(
        contract(patterns[2], values, inner_table), twist_real, -twist_imag
    ).astype(jnp.bfloat16)


def inverse_axis(values, tables, patterns, trailing):
    section_one = inverse_first(values, tables, patterns, trailing)
    return contract(patterns[3], section_one, tables[0]) * (1.0 / table_length(tables))


def window_matrix(half_width):
    positions = jnp.arange(XTILES, dtype=jnp.int32)
    difference = (positions[:, None] - positions[None, :]) % XTILES
    distance = jnp.minimum(difference, XTILES - difference)
    return (distance <= half_width).astype(jnp.float32)


def tile_statistics(first_moment, second_moment, half_width, tile_rows):
    window_mask = window_matrix(half_width)
    cells = ((2 * half_width + 1) * (TILE_X * tile_rows)).astype(jnp.float32)
    mean_one = jnp.dot(first_moment, window_mask, precision=lax.Precision.HIGHEST) / cells
    mean_two = jnp.dot(second_moment, window_mask, precision=lax.Precision.HIGHEST) / cells
    fluctuation = mean_two / (mean_one * mean_one + tiny_value) - 1.0
    return (fluctuation, mean_one * jnp.exp(-fluctuation))


def propagate_columns(phase_patch, tables_y, slant_factor, fresnel_y):
    patch_rows = phase_patch.shape[0]
    width_here = phase_patch.shape[1]
    outer_len = tables_y[0].shape[2]
    inner_len = tables_y[1].shape[2]
    turned_phase = slant_factor * phase_patch
    screen_field = jnp.stack([jnp.cos(turned_phase), jnp.sin(turned_phase)]).astype(jnp.bfloat16)
    stacked = screen_field.reshape(2, outer_len, inner_len, width_here)
    spectral = forward_axis(stacked, tables_y, fresnel_y, column_patterns, True)
    result = inverse_axis(spectral, tables_y, column_patterns, True)
    return result.astype(jnp.bfloat16).reshape(2, patch_rows, width_here)


def half_screen_rows(white_noise, row_start, tables):
    rows_here = white_noise.shape[1]
    row_ids = row_start + jnp.arange(rows_here, dtype=jnp.int32)
    column_ids = jnp.arange(N, dtype=jnp.int32)
    spectral_gain = spectral_filter(row_ids, column_ids)
    spectrum = (white_noise.astype(jnp.float32) * spectral_gain).astype(jnp.bfloat16)
    half_screen = inverse_axis(
        spectrum.reshape(2, rows_here, FIRST, SECOND), tables, row_patterns, False
    )
    half_screen = half_screen.astype(jnp.bfloat16).reshape(2, rows_here, N)
    return half_screen


def gathered_patch(half_screen, geometry, tables, patch_len):
    turned = lax.all_to_all(half_screen, "row", split_axis=2, concat_axis=1, tiled=True)
    band_rows = turned.shape[1]
    columns = turned.shape[2]
    offset_rows = N // 4 * geometry[0, 1]
    blocks = band_rows // SECOND
    block_start = lax.axis_index("dir") * blocks
    stacked = turned.reshape(2, blocks, SECOND, columns)
    twist_real = lax.dynamic_slice_in_dim(tables[2], block_start, blocks, 0)[..., None]
    twist_imag = lax.dynamic_slice_in_dim(tables[3], block_start, blocks, 0)[..., None]
    section_one = complex_times(
        contract("zkcx,wzbc->wkbx", stacked, tables[1]), twist_real, -twist_imag
    )
    section_one = section_one.astype(jnp.bfloat16)
    outer_count = patch_len // SECOND
    outer_ids = (offset_rows // SECOND + jnp.arange(outer_count, dtype=jnp.int32)) % FIRST
    patch_outer = jnp.take(tables[0][0], outer_ids, axis=1)
    phase_patch = contract(
        "zkbx,zak->abx", lax.all_gather(section_one, "dir", axis=1, tiled=True), patch_outer
    )
    return phase_patch.reshape(patch_len, columns) * (1.0 / N)


def host_tables():
    def block(length):
        ids = np.arange(length)
        angle = (ids[:, None] * ids[None, :] % length) * (full_turn / length)
        real_part, imag_part = (np.cos(angle), np.sin(angle))
        return np.array([[real_part, -imag_part], [imag_part, real_part]])

    inner = block(SECOND).transpose(1, 3, 0, 2).reshape(2 * SECOND, 2 * SECOND)
    outer = block(FIRST).transpose(0, 2, 1, 3).reshape(2 * FIRST, 2 * FIRST)
    spread = np.kron(outer, np.eye(GROUP))
    twist = np.arange(FIRST)[:, None] * np.arange(SECOND)[None, :] * (full_turn / N)
    twist = np.repeat(twist, GROUP, axis=0)
    angle = (np.arange(SECOND)[:, None] * np.arange(SECOND)[None, :] % SECOND) * (full_turn / SECOND)
    return (
        inner.astype(ml_dtypes.bfloat16),
        np.stack([np.cos(twist), np.sin(twist)]).astype(np.float32),
        spread.astype(ml_dtypes.bfloat16),
        np.stack([np.cos(angle), np.sin(angle)]).astype(np.float32),
    )


def screen_kernel(
    spot, noise, rows_squared, columns_squared, inner, twist, spread, kept, moved, staged
):
    core, y_spot = (spot[0], spot[1])
    root = lax.rsqrt(16.0 + rows_squared[...] + columns_squared[...])
    gain = strength * root * (root * lax.rsqrt(root))
    spectrum = [noise[z].astype(jnp.float32) * gain for z in range(2)]
    sections = []
    for group in range(2):
        rows = slice(group * GROUP, (group + 1) * GROUP)
        parts = [
            jnp.concatenate(
                [spectrum[z][rows, k * SECOND : (k + 1) * SECOND] for k in range(FIRST)], axis=0
            ).astype(jnp.bfloat16)
            for z in range(2)
        ]
        first = jnp.dot(
            jnp.concatenate(parts, axis=1), inner[...], preferred_element_type=jnp.float32
        )
        real_part, imag_part = (first[:, :SECOND], first[:, SECOND:])
        turned = jnp.concatenate(
            [
                real_part * twist[0] - imag_part * twist[1],
                real_part * twist[1] + imag_part * twist[0],
            ],
            axis=0,
        )
        sections.append(turned.astype(jnp.bfloat16))
    staged[...] = jnp.dot(
        spread[...], jnp.concatenate(sections, axis=1), preferred_element_type=jnp.float32
    )
    for core_side, target in enumerate((kept, moved)):
        for y_side in range(2):
            for chunk in range(CHUNKS):
                for z_spot in range(4):
                    place = z_spot * 4 + (y_spot ^ y_side) * 2 + (core ^ core_side)
                    for w in range(2):
                        start = (w * FIRST + place * CHUNKS + chunk) * GROUP
                        taken = staged[pl.ds(pl.multiple_of(start, GROUP), GROUP), :]
                        both = jnp.concatenate([taken[:, :SECOND], taken[:, SECOND:]], axis=0)
                        target[y_side, chunk, w, :, z_spot * SECOND : (z_spot + 1) * SECOND] = (
                            both.astype(jnp.bfloat16)
                        )


def half_screens(white_noise, row_start, row, host):
    rows_here = white_noise.shape[1]
    inner, twist, spread, _ = host
    row_waves = signed_wave(row_start + jnp.arange(rows_here, dtype=jnp.int32), FIRST, SECOND)
    column_waves = signed_wave(jnp.arange(N, dtype=jnp.int32), FIRST, SECOND)
    spot = jnp.stack([row % 2, row // 2 % 2])
    step = 2 * GROUP
    out_shape = (2, CHUNKS, 2, rows_here, 4 * SECOND)
    out_spec = pl.BlockSpec((2, CHUNKS, 2, step, 4 * SECOND), lambda i: (0, 0, 0, i, 0))

    def whole(array):
        return pl.BlockSpec(array.shape, lambda i: (0,) * array.ndim)

    return pl.pallas_call(
        screen_kernel,
        grid=(rows_here // step,),
        in_specs=[
            pl.BlockSpec(memory_space=pltpu.SMEM),
            pl.BlockSpec((2, step, N), lambda i: (0, i, 0)),
            pl.BlockSpec((step, 1), lambda i: (i, 0)),
            pl.BlockSpec((1, N), lambda i: (0, 0)),
            whole(inner),
            whole(twist),
            whole(spread),
        ],
        out_specs=[out_spec, out_spec],
        out_shape=[jax.ShapeDtypeStruct(out_shape, jnp.bfloat16)] * 2,
        scratch_shapes=[pltpu.VMEM((2 * FIRST * GROUP, 2 * SECOND), jnp.float32)],
        compiler_params=pltpu.CompilerParams(vmem_limit_bytes=48 * 1024 * 1024),
        cost_estimate=pl.CostEstimate(
            flops=20_000_000_000, bytes_accessed=20_000_000, transcendentals=4_000_000
        ),
    )(
        spot,
        white_noise,
        (row_waves * row_waves)[:, None],
        (column_waves * column_waves)[None, :],
        inner,
        twist,
        spread,
    )


def matrix_kernel(slow, fast, matrix):
    for outer in range(matrix.shape[0] // SECOND):
        rows = slice(outer * SECOND, (outer + 1) * SECOND)
        for source in range(2):
            for near in range(2):
                block = source * 2 + near
                slow_real = slow[0, rows, block : block + 1]
                slow_imag = slow[1, rows, block : block + 1]
                real_part = slow_real * fast[0] - slow_imag * fast[1]
                imag_part = slow_real * fast[1] + slow_imag * fast[0]
                for z, part in enumerate((real_part, -imag_part)):
                    start = ((source * 2 + z) * 2 + near) * SECOND
                    matrix[rows, start : start + SECOND] = part.astype(jnp.bfloat16)


def patch_matrix(slant_bins, block_ids, outer_count, fast):
    inner_ids = jnp.arange(SECOND, dtype=jnp.int32)
    outer_ids = slant_bins[:, None] * (FIRST // 4) + jnp.arange(outer_count, dtype=jnp.int32)
    position = (outer_ids[:, :, None] * SECOND + inner_ids).reshape(-1)
    slow = (position[:, None] * block_ids[None, :] % N).astype(jnp.float32) * (full_turn / N)
    slow = jnp.stack([jnp.cos(slow), jnp.sin(slow)])
    length = position.shape[0]
    return pl.pallas_call(
        matrix_kernel,
        grid=(2,),
        in_specs=[
            pl.BlockSpec((2, length // 2, 4), lambda i: (0, i, 0)),
            pl.BlockSpec(fast.shape, lambda i: (0, 0, 0)),
        ],
        out_specs=pl.BlockSpec((length // 2, 8 * SECOND), lambda i: (i, 0)),
        out_shape=jax.ShapeDtypeStruct((length, 8 * SECOND), jnp.bfloat16),
        cost_estimate=pl.CostEstimate(
            flops=8_000_000, bytes_accessed=4_000_000, transcendentals=0
        ),
    )(slow, fast)


def product_kernel(matrix, kept, received, result):
    depth = kept.shape[0] * kept.shape[1]
    columns = kept.shape[2]
    total = jnp.dot(
        matrix[:, :depth],
        kept[...].reshape(depth, columns),
        preferred_element_type=jnp.float32,
    )
    total += jnp.dot(
        matrix[:, depth:],
        received[...].reshape(depth, columns),
        preferred_element_type=jnp.float32,
    )
    result[...] = total.astype(result.dtype).reshape(result.shape)


def patch_products(matrix, kept, received):
    patch_len = matrix.shape[0] // 2
    sides, chunks, parts, rows, columns = kept.shape
    values_spec = pl.BlockSpec(
        (None, None, parts, rows, columns), lambda i, j: (j, i, 0, 0, 0)
    )
    return pl.pallas_call(
        product_kernel,
        grid=(chunks, sides),
        in_specs=[
            pl.BlockSpec(matrix.shape, lambda i, j: (0, 0)),
            values_spec,
            values_spec,
        ],
        out_specs=pl.BlockSpec(
            (None, 2, None, patch_len, columns), lambda i, j: (i, 0, j, 0, 0)
        ),
        out_shape=jax.ShapeDtypeStruct((chunks, 2, sides, patch_len, columns), jnp.bfloat16),
        compiler_params=pltpu.CompilerParams(vmem_limit_bytes=32 * 1024 * 1024),
        cost_estimate=pl.CostEstimate(
            flops=9_000_000_000, bytes_accessed=20_000_000, transcendentals=0
        ),
    )(matrix, kept, received)


def reduce_kernel(
    products, result, a_recv, b_send, b_recv, z_send, z_recv, a_sems, b_sems, z_sems
):
    here_x, row = (lax.axis_index("dir"), lax.axis_index("row"))
    z_spot, y_spot = (row // 4, row // 2 % 2)
    x_mate = (1 - here_x, row)
    y_mate = (here_x, row + 2 - 4 * y_spot)
    z_spots = [(z_spot + shift) % 4 for shift in range(1, 4)]
    z_mates = [(here_x, row + 4 * (spot - z_spot)) for spot in z_spots]
    mates = [x_mate, y_mate] + z_mates
    barrier = pltpu.get_barrier_semaphore()
    for mate in mates:
        pl.semaphore_signal(barrier, inc=1, device_id=mate, device_id_type=pl.DeviceIdType.MESH)
    pl.semaphore_wait(barrier, len(mates))

    height = a_recv.shape[2]
    units = [
        (2 * pair + way, half) for pair in range(2) for half in range(2) for way in range(2)
    ]

    def copy(source, target, sems, spot, mate):
        return pltpu.make_async_remote_copy(
            src_ref=source,
            dst_ref=target,
            send_sem=sems.at[(0, *spot)],
            recv_sem=sems.at[(1, *spot)],
            device_id=mate,
            device_id_type=pl.DeviceIdType.MESH,
        )

    def rows_of(unit):
        return pl.ds(units[unit][1] * height, height)

    a_copies, b_copies, z_copies = ([], [], [])
    for unit, (chunk, _) in enumerate(units):
        rows = rows_of(unit)
        if chunk % 2 == 0:
            source = products.at[chunk, 1, :, rows, :]
            first_mate, second_mate = (x_mate, y_mate)
        else:
            source = products.at[chunk, :, 1, rows, :]
            first_mate, second_mate = (y_mate, x_mate)
        a_copies.append(copy(source, a_recv.at[unit], a_sems, (unit,), first_mate))
        b_copies.append(copy(b_send.at[unit], b_recv.at[unit], b_sems, (unit,), second_mate))
        z_copies.append(
            [
                copy(
                    z_send.at[unit, z_spots[shift]],
                    z_recv.at[unit, shift],
                    z_sems,
                    (unit, shift),
                    z_mates[shift],
                )
                for shift in range(3)
            ]
        )

    def finish(unit):
        chunk, _ = units[unit]
        b_copies[unit].wait_recv()
        total = (
            products[chunk, 0, 0, rows_of(unit), :].astype(jnp.float32)
            + a_recv[unit, 0].astype(jnp.float32)
            + b_recv[unit].astype(jnp.float32)
        ).astype(jnp.bfloat16)
        for spot in range(4):
            z_send[unit, spot] = total[:, spot * SECOND : (spot + 1) * SECOND]
        for sent in z_copies[unit]:
            sent.start()

    count = len(units)
    ahead = 2
    for unit in range(ahead):
        a_copies[unit].start()
    for unit, (chunk, _) in enumerate(units):
        if unit >= 2:
            finish(unit - 2)
        a_copies[unit].wait_recv()
        side = (0, 1) if chunk % 2 == 0 else (1, 0)
        b_send[unit] = (
            products[chunk, side[0], side[1], rows_of(unit), :].astype(jnp.float32)
            + a_recv[unit, 1].astype(jnp.float32)
        ).astype(jnp.bfloat16)
        b_copies[unit].start()
        if unit + ahead < count:
            a_copies[unit + ahead].start()
    finish(count - 2)
    finish(count - 1)
    for unit, (chunk, _) in enumerate(units):
        total = z_send[unit, z_spot].astype(jnp.float32)
        for shift in range(3):
            z_copies[unit][shift].wait_recv()
            total += z_recv[unit, shift].astype(jnp.float32)
        result[rows_of(unit), chunk * SECOND : (chunk + 1) * SECOND] = total
    for unit in range(count):
        a_copies[unit].wait_send()
        b_copies[unit].wait_send()
        for sent in z_copies[unit]:
            sent.wait_send()


def reduce_products(products):
    chunks, _, _, patch_len, columns = products.shape
    count, height = (2 * chunks, patch_len // 2)
    held = jnp.bfloat16
    return pl.pallas_call(
        reduce_kernel,
        in_specs=[pl.BlockSpec(memory_space=pltpu.VMEM)],
        out_specs=pl.BlockSpec(memory_space=pltpu.VMEM),
        out_shape=jax.ShapeDtypeStruct((patch_len, chunks * SECOND), jnp.float32),
        scratch_shapes=[
            pltpu.VMEM((count, 2, height, columns), held),
            pltpu.VMEM((count, height, columns), held),
            pltpu.VMEM((count, height, columns), held),
            pltpu.VMEM((count, 4, height, SECOND), held),
            pltpu.VMEM((count, 3, height, SECOND), held),
            pltpu.SemaphoreType.DMA((2, count)),
            pltpu.SemaphoreType.DMA((2, count)),
            pltpu.SemaphoreType.DMA((2, count, 3)),
        ],
        compiler_params=pltpu.CompilerParams(
            collective_id=0, has_side_effects=True, vmem_limit_bytes=40 * 1024 * 1024
        ),
    )(products)


def reduced_patch(white_noise, row_start, geometry):
    row_count = lax.axis_size("row")
    patch_len = row_count * ROWS_DEV
    row = lax.axis_index("row")
    over_core = [(r, r ^ 1) for r in range(row_count)]
    host = host_tables()
    kept, moved = half_screens(white_noise, row_start, row, host)
    received = lax.ppermute(moved, "row", over_core)
    slant_bin, kept = lax.optimization_barrier((geometry[0, 1], kept))
    other_bin = lax.ppermute(slant_bin, "dir", [(0, 1), (1, 0)])
    first_block = 2 * (lax.axis_index("dir") * row_count + row)
    other_block = 2 * (lax.axis_index("dir") * row_count + (row ^ 1))
    block_ids = jnp.stack([first_block, first_block + 1, other_block, other_block + 1])
    slant_bins = jnp.stack([slant_bin, other_bin])
    matrix = patch_matrix(slant_bins, block_ids, patch_len // SECOND, host[3])
    return reduce_products(patch_products(matrix, kept, received))


def turn_kernel(field, result, landed, local_sem, sems):
    here_dir, row = (lax.axis_index("dir"), lax.axis_index("row"))
    count = lax.axis_size("row")
    height = result.shape[1]
    columns = field.shape[2]
    mates = [(here_dir, (row + shift) % count) for shift in range(1, count)]
    barrier = pltpu.get_barrier_semaphore()
    for mate in mates:
        pl.semaphore_signal(barrier, inc=1, device_id=mate, device_id_type=pl.DeviceIdType.MESH)
    pl.semaphore_wait(barrier, len(mates))
    mine = pl.ds(pl.multiple_of(row * columns, columns), columns)

    def rows_of(spot):
        return pl.ds(pl.multiple_of(spot * height, height), height)

    copies = [
        pltpu.make_async_remote_copy(
            src_ref=field.at[:, rows_of(mate[1]), :],
            dst_ref=landed.at[:, :, mine],
            send_sem=sems.at[0, spot],
            recv_sem=sems.at[1, spot],
            device_id=mate,
            device_id_type=pl.DeviceIdType.MESH,
        )
        for spot, mate in enumerate(mates)
    ]
    for sent in copies:
        sent.start()
    local = pltpu.make_async_copy(field.at[:, rows_of(row), :], landed.at[:, :, mine], local_sem)
    local.start()
    local.wait()
    for sent in copies:
        sent.wait_recv()
    result[...] = landed[...]
    for sent in copies:
        sent.wait_send()


def turn_field(field):
    count = lax.axis_size("row")
    parts, patch_len, columns = field.shape
    shape = (parts, patch_len // count, count * columns)
    return pl.pallas_call(
        turn_kernel,
        in_specs=[pl.BlockSpec(memory_space=pltpu.VMEM)],
        out_specs=pl.BlockSpec(memory_space=pltpu.VMEM),
        out_shape=jax.ShapeDtypeStruct(shape, field.dtype),
        scratch_shapes=[
            pltpu.VMEM(shape, field.dtype),
            pltpu.SemaphoreType.DMA,
            pltpu.SemaphoreType.DMA((2, count - 1)),
        ],
        compiler_params=pltpu.CompilerParams(
            collective_id=1, has_side_effects=True, vmem_limit_bytes=16 * 1024 * 1024
        ),
    )(field)


def share_kernel(terms, result, landed, planes, landed_planes, sems, plane_sems):
    here_dir, row = (lax.axis_index("dir"), lax.axis_index("row"))
    plane, low = (row // 4, row % 4)
    count, depth = (terms.shape[0], terms.shape[1])
    here = here_dir * 4 + low
    spots = [(here + shift) % count for shift in range(1, count)]
    mates = [(spot // 4, plane * 4 + spot % 4) for spot in spots]
    plane_spots = [(plane + shift) % depth for shift in range(1, depth)]
    plane_mates = [(here_dir, spot * 4 + low) for spot in plane_spots]
    barrier = pltpu.get_barrier_semaphore()
    for mate in mates + plane_mates:
        pl.semaphore_signal(barrier, inc=1, device_id=mate, device_id_type=pl.DeviceIdType.MESH)
    pl.semaphore_wait(barrier, len(mates) + len(plane_mates))

    def exchange(source, target, semaphores, places, devices):
        copies = [
            pltpu.make_async_remote_copy(
                src_ref=source.at[spot],
                dst_ref=target.at[place],
                send_sem=semaphores.at[0, place],
                recv_sem=semaphores.at[1, place],
                device_id=mate,
                device_id_type=pl.DeviceIdType.MESH,
            )
            for place, (spot, mate) in enumerate(zip(places, devices))
        ]
        for sent in copies:
            sent.start()
        return copies

    copies = exchange(terms, landed, sems, spots, mates)
    total = terms[here]
    for place, sent in enumerate(copies):
        sent.wait_recv()
        total += landed[place]
    planes[...] = total
    plane_copies = exchange(planes, landed_planes, plane_sems, plane_spots, plane_mates)
    total = planes[plane]
    for place, sent in enumerate(plane_copies):
        sent.wait_recv()
        total += landed_planes[place]
    result[...] = total
    for sent in copies + plane_copies:
        sent.wait_send()


def share_sums(terms):
    lanes = terms.shape[2]
    count, depth = (8, terms.shape[0] // 8)
    ordered = terms.reshape(2, depth, 4, 1, lanes).transpose(0, 2, 1, 3, 4)
    ordered = ordered.reshape(count, depth, 1, lanes)
    return pl.pallas_call(
        share_kernel,
        in_specs=[pl.BlockSpec(memory_space=pltpu.VMEM)],
        out_specs=pl.BlockSpec(memory_space=pltpu.VMEM),
        out_shape=jax.ShapeDtypeStruct((1, lanes), terms.dtype),
        scratch_shapes=[
            pltpu.VMEM((count - 1, depth, 1, lanes), terms.dtype),
            pltpu.VMEM((depth, 1, lanes), terms.dtype),
            pltpu.VMEM((depth - 1, 1, lanes), terms.dtype),
            pltpu.SemaphoreType.DMA((2, count - 1)),
            pltpu.SemaphoreType.DMA((2, depth - 1)),
        ],
        compiler_params=pltpu.CompilerParams(collective_id=2, has_side_effects=True),
    )(ordered)


def body(white_noise, geometry, window, tile_map, link_gain, serving):
    row_count = lax.axis_size("row")
    tables = transform_tables(FIRST, SECOND)
    tables_y = transform_tables(row_count, ROWS_DEV)
    patch_len = row_count * ROWS_DEV
    rows_here = white_noise.shape[1]
    row_start = lax.axis_index(("dir", "row")) * rows_here
    slant_factor = 1.0 + 0.25 * geometry[0, 1].astype(jnp.float32)
    fresnel_x = fresnel_factor(geometry[0], FIRST, SECOND)
    fresnel_y = fresnel_factor(geometry[0], row_count, ROWS_DEV)
    direct = lax.axis_size("dir") == 2 and row_count == 16 and rows_here == 2 * SECOND
    if direct:
        phase_patch = reduced_patch(white_noise, row_start, geometry)
    else:
        half_screen = half_screen_rows(white_noise, row_start, tables)
        phase_patch = gathered_patch(half_screen, geometry, tables, patch_len)
    columns = phase_patch.shape[1]
    screen_field = propagate_columns(phase_patch, tables_y, slant_factor, fresnel_y)
    if direct:
        portion = turn_field(screen_field)[:, None]
    else:
        stacked_field = screen_field.reshape(2, row_count, ROWS_DEV, columns)
        portion = lax.all_to_all(stacked_field, "row", split_axis=1, concat_axis=3, tiled=True)
    item_count = portion.shape[2]
    stacked = portion.reshape(2, item_count, FIRST, SECOND)
    spectral = forward_axis(stacked, tables, fresnel_x, row_patterns, False)
    wave_field = inverse_axis(spectral, tables, row_patterns, False)
    intensity = wave_field[0] * wave_field[0] + wave_field[1] * wave_field[1]
    intensity = intensity.reshape(item_count, XTILES, TILE_X)
    tile_one = jnp.sum(intensity, axis=2)
    tile_two = jnp.sum(intensity * intensity, axis=2)
    tile_rows = ROWS_DEV // YTILES
    first_moment = jnp.sum(tile_one.reshape(YTILES, tile_rows, XTILES), axis=1)
    second_moment = jnp.sum(tile_two.reshape(YTILES, tile_rows, XTILES), axis=1)
    fluctuation, faded_power = tile_statistics(first_moment, second_moment, window[0], tile_rows)
    faded_flat = faded_power.reshape(-1)
    tile_total = faded_flat.shape[0]
    local_tile = tile_map[0] - lax.axis_index("row") * tile_total
    inside = (local_tile >= 0) & (local_tile < tile_total)
    looked = jnp.where(inside, jnp.take(faded_flat, jnp.clip(local_tile, 0, tile_total - 1)), 0.0)
    received = link_gain[0] * looked
    direction = lax.axis_index("dir")
    serves_here = serving == direction
    signal_part = jnp.where(serves_here, received, 0.0)
    interference_part = jnp.where(serves_here, 0.0, received)
    device_count = lax.axis_size(("dir", "row"))
    terms = jnp.stack([signal_part, interference_part]).reshape(2, device_count, -1)
    if direct:
        share = terms.shape[2]
        padded = jnp.pad(
            terms.transpose(1, 0, 2).reshape(device_count, 1, 2 * share),
            ((0, 0), (0, 0), (0, SECOND - 2 * share)),
        )
        summed = share_sums(padded)[0]
        signal, interference = (summed[:share], summed[share : 2 * share])
    else:
        gathered = lax.all_to_all(
            terms.transpose(1, 0, 2), ("dir", "row"), split_axis=0, concat_axis=0, tiled=True
        )
        signal, interference = jnp.sum(gathered, axis=0)
    signal_ratio = jnp.log10(signal / (interference + noise_floor))
    return (fluctuation[None], signal_ratio)


def solution(mesh):
    return jax.shard_map(
        body,
        mesh=mesh,
        in_specs=(
            P(None, ("dir", "row"), None),
            P("dir", None),
            P("dir"),
            P("dir", None),
            P("dir", None),
            P(),
        ),
        out_specs=(P("dir", "row", None), P(("dir", "row"))),
        check_vma=False,
    )
```
